128 devices in a mesh: frame: 8 (over x, z_hi), pos: 16 (over y, z_lo, core).
Axes of the slice: x: 4, y: 4, z: 4 (z_hi: 2, z_lo: 2; z = z_hi * 2 + z_lo), core: 2. Of those that a mesh axis runs over, the one named last changes fastest.
Arguments:
- tokens: bfloat16 [64, 1024, 1152], P('frame', 'pos'), may hold values from -6 to 6
- frame_valid: int32 [64], replicated, may hold values from 0 to 1, as said below
- text: bfloat16 [300, 1152], replicated, may hold values from -6 to 6
- modulation: float32 [6, 1152], replicated, may hold values from -4 to 4
- qk_gains: float32 [4, 72], replicated, may hold values from 0.8 to 4.5, as said below
- spatial_qkv: bfloat16 [1152, 3456], replicated
- spatial_out: bfloat16 [1152, 1152], replicated, may hold values from -0.1875 to 0.1875
- block_weights: bfloat16 [1152, 6912], P('frame')
- cross_kv: bfloat16 [1152, 2, 1152], P(None, None, 'pos'), may hold values from -0.1875 to 0.1875
Outputs:
- mixed: bfloat16 [64, 1024, 1152], P('frame', 'pos')
The draws below stay inside these ranges and needn't reach their ends.
Inputs may be any that keep to these rules, and one draw needn't show every extreme that they name: `frame_valid`: 1 for a leading run of frames and 0 after it; frame 0 is always 1, the last frame always 0, and at least 16 frames are 1. `qk_gains`: positive.
All inputs are finite; a program needn't handle non-finite values.
Results may differ from the reference program's by a relative error of at most 0.02.
Values may be sent and summed in bfloat16 or wider, within the bound.
No kernel may reach another device: no remote copies, remote signals or barrier semaphores. Data moves between devices by JAX's collectives and lax.ppermute only.
A program may use at most 320 MiB of HBM per device.

```python
import jax
import jax.numpy as jnp
from jax import lax

D = 1152
HEADS = 16
HD = 72
LEN = 300
F = 64
P_SIZE = 1024


def draw_frame_valid(key, part):
    key = jax.random.fold_in(key, 3)
    count = jax.random.randint(key, (), F // 4, F)
    return (jnp.arange(F) < count).astype(jnp.int32)


def draw_qk_gains(key, part):
    key = jax.random.fold_in(key, 5)
    return jnp.exp(jax.random.uniform(key, (4, HD), jnp.float32, jnp.log(0.8), jnp.log(2.0)))


def tied_columns(key, count):
    weight = jax.random.normal(key, (D, count * D), jnp.float32) * D ** (-0.5)
    return weight


def draw_spatial_qkv(key, part):
    key = jax.random.fold_in(key, 7)
    return tied_columns(key, 3).astype(jnp.bfloat16)


def draw_block_weights(key, part):
    key = jax.random.fold_in(key, 11)
    return tied_columns(key, 6).astype(jnp.bfloat16)


def steps_of(own_key, dims, cuts, least, largest):
    def one(position, parts):
        steps = jax.random.uniform(jax.random.fold_in(jax.random.fold_in(own_key, 6), position), (parts,), jnp.float32, least / len(cuts), largest / len(cuts))
        return jnp.repeat(jnp.exp(steps), dims[position] // parts).reshape((-1,) + (1,) * (len(dims) - position - 1))

    level = one(*cuts[0])
    for cut in cuts[1:]:
        level = level * one(*cut)
    return level


def scatter_about(stream_key, dims, spread, limit, cuts=(), dtype=jnp.bfloat16):
    entries = spread * jax.random.normal(stream_key, dims, jnp.float32)
    if cuts:
        entries = entries * steps_of(stream_key, dims, cuts, -0.22, 0.18)
    return jnp.clip(entries, -limit, limit).astype(dtype)


def setup_inputs(seed: int = 0) -> dict:
    streams_of = jax.random.split(jax.random.key(seed), 10)
    return {
        "tokens": scatter_about(streams_of[0], (F, P_SIZE, D), 1.0, 6.0, ((0, 8), (1, 16))),
        "frame_valid": draw_frame_valid(jax.random.fold_in(streams_of[9], 71), 0),
        "text": scatter_about(streams_of[2], (LEN, D), 1.0, 6.0),
        "modulation": scatter_about(streams_of[3], (6, D), 0.7, 4.0, (), jnp.float32),
        "qk_gains": draw_qk_gains(jax.random.fold_in(streams_of[9], 71), 0),
        "spatial_qkv": draw_spatial_qkv(jax.random.fold_in(streams_of[9], 71), 0),
        "spatial_out": scatter_about(streams_of[6], (D, D), D ** -0.5, 0.1875),
        "block_weights": draw_block_weights(jax.random.fold_in(streams_of[9], 71), 0),
        "cross_kv": scatter_about(streams_of[8], (D, 2, D), D ** -0.5, 0.1875, ((2, 16),)),
    }


def layer_norm(values):
    mean = lax.optimization_barrier(jnp.mean(values, -1, keepdims=True))
    centred = values - mean
    return centred * lax.rsqrt(lax.optimization_barrier(jnp.mean(centred * centred, -1, keepdims=True)) + 1e-06)

def modulate(values, shift, scale):
    return layer_norm(values.astype(jnp.float32)) * (1.0 + scale) + shift

def head_norm(values, gain):
    return values * lax.rsqrt(lax.optimization_barrier(jnp.mean(values * values, -1, keepdims=True)) + 1e-06) * gain

def widen(values):
    return lax.optimization_barrier(values).astype(jnp.float32)

def project(inputs, weight, gain_q, gain_k):
    lead = inputs.shape[:-1]
    width = weight.shape[1] // 3
    mixed = jnp.dot(inputs.reshape(-1, inputs.shape[-1]), weight, preferred_element_type=jnp.float32)
    query = head_norm(mixed[:, :width].reshape(-1, HEADS, HD), gain_q).astype(jnp.bfloat16)
    keys = head_norm(mixed[:, width:2 * width].reshape(-1, HEADS, HD), gain_k).astype(jnp.bfloat16)
    values = mixed[:, 2 * width:].reshape(-1, HEADS, HD).astype(jnp.bfloat16)
    shape = lead + (HEADS, HD)
    return (query.reshape(shape), keys.reshape(shape), values.reshape(shape))

def frame_attention(triple):
    query, keys, values = triple
    scores = jnp.einsum('qhd,khd->hqk', widen(query), widen(keys)) * HD ** (-0.5)
    expo = jnp.exp(scores - lax.optimization_barrier(jnp.max(scores, -1, keepdims=True)))
    total = lax.optimization_barrier(jnp.sum(expo, -1))
    out = jnp.einsum('hqk,khd->qhd', widen(expo.astype(jnp.bfloat16)), widen(values))
    return (out / total.T[:, :, None]).astype(jnp.bfloat16)

def reference(tokens, frame_valid, text, modulation, qk_gains, spatial_qkv, spatial_out, block_weights, cross_kv):
    frames, places, width = tokens.shape
    spatial_in = modulate(tokens, modulation[0], modulation[1]).astype(jnp.bfloat16)
    query, keys, values = project(spatial_in, spatial_qkv, qk_gains[0], qk_gains[1])
    spatial_attn = lax.map(frame_attention, (query, keys, values))
    proj = jnp.dot(spatial_attn.reshape(-1, width), spatial_out, preferred_element_type=jnp.float32)
    after_spatial = (tokens.astype(jnp.float32) + modulation[2] * proj.reshape(tokens.shape)).astype(jnp.bfloat16)
    temporal_in = modulate(after_spatial, modulation[3], modulation[4]).astype(jnp.bfloat16)
    query, keys, values = project(temporal_in, block_weights[:, :3 * width], qk_gains[2], qk_gains[3])
    valid = (frame_valid > 0)[None, None, None, :]
    scores = jnp.einsum('qphd,kphd->phqk', widen(query), widen(keys)) * HD ** (-0.5)
    scores = jnp.where(valid, scores, -1e+30)
    expo = jnp.where(valid, jnp.exp(scores - lax.optimization_barrier(jnp.max(scores, -1, keepdims=True))), 0.0)
    total = lax.optimization_barrier(jnp.sum(expo, -1))
    out = jnp.einsum('phqk,kphd->qphd', widen(expo.astype(jnp.bfloat16)), widen(values))
    temporal_attn = (out / jnp.transpose(total, (2, 0, 1))[:, :, :, None]).astype(jnp.bfloat16)
    proj = jnp.dot(temporal_attn.reshape(-1, width), block_weights[:, 3 * width:4 * width], preferred_element_type=jnp.float32)
    after_temporal = (after_spatial.astype(jnp.float32) + modulation[5] * proj.reshape(tokens.shape)).astype(jnp.bfloat16)
    cross_q = jnp.dot(after_temporal.reshape(-1, width), block_weights[:, 4 * width:5 * width], preferred_element_type=jnp.float32)
    cross_q = cross_q.astype(jnp.bfloat16).reshape(frames, places, HEADS, HD)
    text_kv = jnp.einsum('ld,dce->lce', text.astype(jnp.float32), cross_kv.astype(jnp.float32)).astype(jnp.bfloat16)
    text_keys = text_kv[:, 0].reshape(-1, HEADS, HD)
    text_values = text_kv[:, 1].reshape(-1, HEADS, HD)

    def cross_frame(query):
        scores = jnp.einsum('qhd,lhd->hql', widen(query), widen(text_keys)) * HD ** (-0.5)
        expo = jnp.exp(scores - lax.optimization_barrier(jnp.max(scores, -1, keepdims=True)))
        total = lax.optimization_barrier(jnp.sum(expo, -1))
        out = jnp.einsum('hql,lhd->qhd', widen(expo.astype(jnp.bfloat16)), widen(text_values))
        return (out / total.T[:, :, None]).astype(jnp.bfloat16)
    cross_attn = lax.map(cross_frame, cross_q)
    proj = jnp.dot(cross_attn.reshape(-1, width), block_weights[:, 5 * width:], preferred_element_type=jnp.float32)
    return (after_temporal.astype(jnp.float32) + proj.reshape(tokens.shape)).astype(jnp.bfloat16)
```

```python
import functools
import jax
import jax.numpy as jnp
from jax import lax
from jax.experimental import pallas as pl
from jax.experimental.pallas import tpu as pltpu

D = 1152
HD = 72
HEADS = 16
WIN = 256
TEXT = 300
TPAD = 304
SAFE = 96.0
BF = jnp.bfloat16
F32 = jnp.float32


def dot(a, b):
    return jnp.dot(a, b, preferred_element_type=F32)


def indicators():
    feature = lax.broadcasted_iota(jnp.int32, (D, 128), 0)
    low = lax.broadcasted_iota(jnp.int32, (D, 128), 1) * HD
    gather = ((feature >= low) & (feature < low + HD)).astype(F32).astype(BF)
    feature = lax.broadcasted_iota(jnp.int32, (256, D), 1)
    low = lax.rem(lax.broadcasted_iota(jnp.int32, (256, D), 0), 128) * HD
    spread = ((feature >= low) & (feature < low + HD)).astype(F32).astype(BF)
    return gather, spread


def norm_rows(x, shift, scale):
    mean = jnp.mean(x, -1, keepdims=True)
    centred = x - mean
    r = lax.rsqrt(jnp.mean(centred * centred, -1, keepdims=True) + 1e-6)
    return (centred * r * (1.0 + scale) + shift).astype(BF)


def head_norm_rows(u, gather, spread, gain):
    total = dot((u * u).astype(BF), gather)
    r = lax.rsqrt(total * (1.0 / HD) + 1e-6)
    high = r.astype(BF)
    low = (r - high.astype(F32)).astype(BF)
    return (u * dot(jnp.concatenate([high, low], -1), spread) * gain).astype(BF)


def window_of(h):
    start = jnp.minimum((h * HD) // 128 * 128, D - WIN)
    return pl.multiple_of(start, 128), h * HD - start


def head_rows(h):
    return pl.ds(pl.multiple_of(h * HD, 8), HD)


def query_of(qt, h, gain):
    start, off = window_of(h)
    win = pl.ds(start, WIN)
    row = lax.broadcasted_iota(jnp.int32, (WIN, 1), 0)
    mine = (row >= off) & (row < off + HD)
    own = qt[head_rows(h), :]
    if gain is None:
        return jnp.where(mine, qt[win, :], 0.0).astype(BF)
    r = lax.rsqrt(jnp.sum(own * own, 0, keepdims=True) * (1.0 / HD) + 1e-6)
    return (jnp.where(mine, qt[win, :], 0.0) * r * gain[win, :]).astype(BF)


def softmax(s, shifted):
    if shifted:
        s = s - jnp.max(s, 0, keepdims=True)
    return jnp.exp2(s).astype(BF)


def values_of(vt, h, cols):
    v = vt[head_rows(h), cols].astype(BF)
    return jnp.concatenate([v, jnp.ones((8, v.shape[1]), BF)], 0)


def loop(n, body):
    def step(i, carry):
        body(i)
        return carry

    lax.fori_loop(0, n, step, 0)


def guarded(gq, gk, run):
    bound = jnp.max(gq[...] * gk[...]) * HD

    @pl.when(bound <= SAFE)
    def _():
        run(False)

    @pl.when(bound > SAFE)
    def _():
        run(True)


def spatial_kernel(own, other, wqkv, wout, mod, gq, gk, gqt, out, xin, k, qt, vt, at, *, rows):
    gather, spread = indicators()
    shift, scale, gate = mod[0:1, :], mod[1:2, :], mod[2:3, :]
    R = 256
    for b in range(rows // R):
        sl = pl.ds(b * R, R)
        xin[sl, :] = norm_rows(own[sl, :].astype(F32), shift, scale)
        xin[pl.ds(rows + b * R, R), :] = norm_rows(other[sl, :].astype(F32), shift, scale)
    for b in range(rows // R):
        sl = pl.ds(b * R, R)
        qt[:, sl] = dot(xin[sl, :], wqkv[:, 0:D]).T
    for b in range(2 * rows // R):
        sl = pl.ds(b * R, R)
        k[sl, :] = head_norm_rows(dot(xin[sl, :], wqkv[:, D:2 * D]), gather, spread, gk[...])
        vt[:, sl] = dot(xin[sl, :], wqkv[:, 2 * D:]).T

    def run(shifted):
        def pair(i):
            for h in (2 * i, 2 * i + 1):
                start, _ = window_of(h)
                q = query_of(qt, h, gqt)
                p = softmax(dot(k[:, pl.ds(start, WIN)], q), shifted)
                o = dot(values_of(vt, h, slice(None)), p)
                at[head_rows(h), :] = o[:HD] * (1.0 / o[HD:HD + 1])

        loop(HEADS // 2, pair)

    guarded(gq, gk, run)
    for b in range(rows // R):
        sl = pl.ds(b * R, R)
        proj = dot(at[:, sl].T.astype(BF), wout[...])
        out[sl, :] = (own[sl, :].astype(F32) + gate * proj).astype(BF)


VMEM = pl.BlockSpec(memory_space=pltpu.VMEM)
PARAMS = pltpu.CompilerParams(vmem_limit_bytes=60 * 2**20)


def spatial(own, other, wqkv, wout, mod, gq, gk, gqt):
    rows = own.shape[0]
    return pl.pallas_call(
        functools.partial(spatial_kernel, rows=rows),
        out_shape=jax.ShapeDtypeStruct((rows, D), BF),
        in_specs=[VMEM] * 8,
        out_specs=VMEM,
        scratch_shapes=[
            pltpu.VMEM((2 * rows, D), BF),
            pltpu.VMEM((2 * rows, D), BF),
            pltpu.VMEM((D, rows), F32),
            pltpu.VMEM((D, 2 * rows), F32),
            pltpu.VMEM((D, rows), F32),
        ],
        compiler_params=PARAMS,
        name="spatial",
    )(own, other, wqkv, wout, mod, gq, gk, gqt)


PART = 1664
REST = 128
SHARD = 144


def piece_copies(place, pieces, weight, sems):
    x, z, c = place[0], place[1], place[2]
    copies = []

    def add(src, shard, column, width, at):
        rows = pl.ds(pl.multiple_of(shard * SHARD, 16), SHARD)
        dst = weight.at[rows, pl.ds(pl.multiple_of(column, 128), width)]
        copies.append(pltpu.make_async_copy(src.at[:, pl.ds(at, width)], dst, sems.at[len(copies)]))

    for core in range(2):
        near, left, right, far0, far1 = pieces[5 * core:5 * core + 5]
        column = PART * (c if core == 0 else 1 - c)
        for dz in range(2):
            zz = z if dz == 0 else 1 - z
            far = far0 if dz == 0 else far1
            for dx, src in ((0, near.at[dz]), (3, left.at[dz]), (1, right.at[dz]), (2, far)):
                shard = 2 * lax.rem(x + dx, 4) + zz
                add(src, shard, column, PART, 0)
                if core == 0:
                    add(src, shard, 2 * PART, REST, PART)
    return copies


def temporal_kernel(place, *refs, rows, frames):
    first, second = refs[:10], refs[10:20]
    x, valid, tk, tvt, mod, gq, gk, gqt, out, w1, w2, xp, xin, k, qt, vt, at, sems = refs[20:]
    copies1 = piece_copies(place, first, w1, sems.at[0])
    copies2 = piece_copies(place, second, w2, sems.at[1])
    for copy in copies1 + copies2:
        copy.start()
    gather, spread = indicators()
    places = rows // frames
    shift, scale, gate = mod[3:4, :], mod[4:5, :], mod[5:6, :]
    R = 256
    group = R // frames
    to = lax.broadcasted_iota(jnp.int32, (rows, rows), 0)
    source = lax.broadcasted_iota(jnp.int32, (rows, rows), 1)
    order = (source == lax.rem(to, frames) * places + to // frames).astype(F32).astype(BF)
    for b in range(rows // R):
        sl = pl.ds(b * R, R)
        moved = dot(order[b * R:(b + 1) * R, :], x[...])
        xp[sl, :] = moved.astype(BF)
        xin[sl, :] = norm_rows(moved, shift, scale)
    for copy in copies1:
        copy.wait()
    for b in range(rows // R):
        sl = pl.ds(b * R, R)
        qt[:, sl] = dot(xin[sl, :], w1[:, 0:D]).T
        k[sl, :] = head_norm_rows(dot(xin[sl, :], w1[:, D:2 * D]), gather, spread, gk[...])
        vt[:, sl] = dot(xin[sl, :], w1[:, 2 * D:]).T

    key = lax.broadcasted_iota(jnp.int32, (R, R), 0) // frames
    query = lax.broadcasted_iota(jnp.int32, (R, R), 1) // frames
    bias = jnp.where(key == query, 0.0, -1e30) + valid[...]

    def run(shifted):
        def pair(i):
            for h in (2 * i, 2 * i + 1):
                start, _ = window_of(h)
                q = query_of(qt, h, gqt)
                for b in range(rows // R):
                    sl = pl.ds(b * R, R)
                    s = dot(k[sl, pl.ds(start, WIN)], q[:, b * R:(b + 1) * R]) + bias
                    o = dot(values_of(vt, h, sl), softmax(s, shifted))
                    at[head_rows(h), sl] = o[:HD] * (1.0 / o[HD:HD + 1])

        loop(HEADS // 2, pair)

    guarded(gq, gk, run)
    for copy in copies2:
        copy.wait()
    for b in range(rows // R):
        sl = pl.ds(b * R, R)
        proj = dot(at[:, sl].T.astype(BF), w2[:, 0:D])
        after = (xp[sl, :].astype(F32) + gate * proj).astype(BF)
        xp[sl, :] = after
        cq = dot(after, w2[:, D:2 * D]).astype(BF).astype(F32) * (HD ** -0.5 * 1.4426950408889634)
        qt[:, sl] = cq.T

    lane = lax.broadcasted_iota(jnp.int32, (8, TPAD), 1)
    ones = (lane < TEXT).astype(F32).astype(BF)

    def pair(i):
        for h in (2 * i, 2 * i + 1):
            start, _ = window_of(h)
            q = query_of(qt, h, None)
            p = softmax(dot(tk[:, pl.ds(start, WIN)], q), True)
            v = jnp.concatenate([tvt[head_rows(h), :].astype(BF), ones], 0)
            o = dot(v, p)
            at[head_rows(h), :] = o[:HD] * (1.0 / o[HD:HD + 1])

    loop(HEADS // 2, pair)
    for b in range(rows // R):
        sl = pl.ds(b * R, R)
        proj = dot(at[:, sl].T.astype(BF), w2[:, 2 * D:])
        xin[sl, :] = (xp[sl, :].astype(F32) + proj).astype(BF)
    to = lax.broadcasted_iota(jnp.int32, (rows, rows), 0)
    source = lax.broadcasted_iota(jnp.int32, (rows, rows), 1)
    groups = frames // 8
    place, frame = lax.rem(to, places), to // places
    held = lax.rem(frame, 8) * groups + frame // 8
    order = (source == place * frames + held).astype(F32).astype(BF)
    for b in range(rows // R):
        sl = pl.ds(b * R, R)
        out[sl, :] = dot(order[b * R:(b + 1) * R, :], xin[...]).astype(BF)


def temporal(place, first, second, x, valid, tk, tvt, mod, gq, gk, gqt):
    rows = x.shape[0]
    hbm = pl.BlockSpec(memory_space=pl.ANY)
    return pl.pallas_call(
        functools.partial(temporal_kernel, rows=rows, frames=64),
        out_shape=jax.ShapeDtypeStruct((rows, D), BF),
        in_specs=[pl.BlockSpec(memory_space=pltpu.SMEM)] + [hbm] * 20 + [VMEM] * 8,
        out_specs=VMEM,
        scratch_shapes=[
            pltpu.VMEM((D, 3 * D), BF),
            pltpu.VMEM((D, 3 * D), BF),
            pltpu.VMEM((rows, D), BF),
            pltpu.VMEM((rows, D), BF),
            pltpu.VMEM((rows, D), BF),
            pltpu.VMEM((D, rows), F32),
            pltpu.VMEM((D, rows), F32),
            pltpu.VMEM((D, rows), F32),
            pltpu.SemaphoreType.DMA((2, 24)),
        ],
        compiler_params=PARAMS,
        name="temporal",
    )(place, *first, *second, x, valid, tk, tvt, mod, gq, gk, gqt)


import numpy as np
from jax.sharding import Mesh, PartitionSpec as P

XZ = ("x", "zh")
YZ = ("y", "zl")
RIGHT = [(i, (i + 1) % 4) for i in range(4)]
LEFT = [(i, (i + 3) % 4) for i in range(4)]
SWAP = [(0, 1), (1, 0)]
ACROSS = [(0, 3), (3, 0), (1, 2), (2, 1)]


def gains(gain_q, gain_k):
    scaled = jnp.tile(gain_q, HEADS) * (HD ** -0.5 * 1.4426950408889634)
    return scaled.reshape(1, D), jnp.tile(gain_k, HEADS).reshape(1, D), scaled.reshape(D, 1)


def weight_pieces(own):
    near = jnp.stack([own, lax.ppermute(own, ("zh", "zl"), ACROSS)])
    left = lax.ppermute(near, "x", RIGHT)
    right = lax.ppermute(near, "x", LEFT)
    far0 = lax.ppermute(left[0], "x", RIGHT)
    far1 = lax.ppermute(right[1], "x", LEFT)
    pieces = (near, left, right, far0, far1)
    return pieces + tuple(lax.ppermute(piece, "c", SWAP) for piece in pieces)


def per_device(tokens, frame_valid, text, modulation, qk_gains, spatial_qkv, spatial_out, block_weights, cross_kv):
    core = lax.axis_index("c")
    groups = []
    for g in range(2):
        base = 3 * D * g
        part = lax.dynamic_slice(block_weights, (0, base + PART * core), (SHARD, PART))
        rest = block_weights[:, base + 2 * PART:base + 3 * D]
        groups.append(jnp.concatenate([part, rest], 1))
    first, second = weight_pieces(groups[0]), weight_pieces(groups[1])
    own = lax.all_to_all(tokens, YZ, 0, 0, tiled=True).reshape(-1, D)
    other = lax.ppermute(own, "c", SWAP)
    local = jnp.dot(text, cross_kv.reshape(D, 2 * HD), preferred_element_type=F32).astype(BF)
    every = lax.all_gather(local, ("y", "zl", "c"), axis=0)
    every = every.reshape(HEADS, TEXT, 2, HD)
    tk = jnp.pad(jnp.transpose(every[:, :, 0], (1, 0, 2)).reshape(TEXT, D), ((0, TPAD - TEXT), (0, 0)), mode="edge")
    tvt = jnp.pad(jnp.transpose(every[:, :, 1], (0, 2, 1)).reshape(D, TEXT), ((0, 0), (0, TPAD - TEXT))).astype(F32)
    after_spatial = spatial(own, other, spatial_qkv, spatial_out, modulation, *gains(qk_gains[0], qk_gains[1]))
    rows = lax.all_to_all(after_spatial.reshape(64, 8, D), YZ + XZ, 0, 0, tiled=True).reshape(-1, D)
    seen = jnp.where(frame_valid.reshape(8, 8).T.reshape(64) > 0, 0.0, -1e30)
    valid = jnp.tile(seen, 4).reshape(256, 1).astype(F32)
    place = jnp.stack([lax.axis_index("x"), lax.axis_index("zh"), core]).astype(jnp.int32)
    mixed = temporal(place, first, second, rows, valid, tk, tvt, modulation, *gains(qk_gains[2], qk_gains[3]))
    back = lax.all_to_all(mixed.reshape(8, 64, D), XZ, 0, 0, tiled=True)
    return jnp.transpose(back.reshape(8, 8, 8, D), (1, 0, 2, 3)).reshape(8, 64, D)


def solution(mesh):
    fine = Mesh(np.asarray(mesh.devices).reshape(4, 2, 4, 2, 2), ("x", "zh", "y", "zl", "c"))
    pos = ("y", "zl", "c")
    placed = (P(XZ, pos, None), P(), P(), P(), P(), P(), P(), P(XZ, None), P(None, None, pos))
    return jax.shard_map(per_device, mesh=fine, in_specs=placed, out_specs=P(XZ, pos, None), check_vma=False)
```

```python
import functools
import jax
import jax.numpy as jnp
from jax import lax
from jax.experimental import pallas as pl
from jax.experimental.pallas import tpu as pltpu

D = 1152
HD = 72
HEADS = 16
WIN = 256
TEXT = 300
TPAD = 304
SHARD = 144
HALF = 80
SAFE = 96.0
BF = jnp.bfloat16
F32 = jnp.float32


def dot(a, b):
    return jnp.dot(a, b, preferred_element_type=F32)


def indicators():
    feature = lax.broadcasted_iota(jnp.int32, (D, 128), 0)
    low = lax.broadcasted_iota(jnp.int32, (D, 128), 1) * HD
    gather = ((feature >= low) & (feature < low + HD)).astype(F32).astype(BF)
    feature = lax.broadcasted_iota(jnp.int32, (256, D), 1)
    low = lax.rem(lax.broadcasted_iota(jnp.int32, (256, D), 0), 128) * HD
    spread = ((feature >= low) & (feature < low + HD)).astype(F32).astype(BF)
    return gather, spread


def norm_rows(x, shift, scale):
    mean = jnp.mean(x, -1, keepdims=True)
    centred = x - mean
    r = lax.rsqrt(jnp.mean(centred * centred, -1, keepdims=True) + 1e-6)
    return (centred * r * (1.0 + scale) + shift).astype(BF)


def head_norm_rows(u, gather, spread, gain):
    total = dot((u * u).astype(BF), gather)
    r = lax.rsqrt(total * (1.0 / HD) + 1e-6)
    high = r.astype(BF)
    low = (r - high.astype(F32)).astype(BF)
    return (u * dot(jnp.concatenate([high, low], -1), spread) * gain).astype(BF)


def window_of(h):
    start = jnp.minimum((h * HD) // 128 * 128, D - WIN)
    return pl.multiple_of(start, 128), h * HD - start


def head_rows(h):
    return pl.ds(pl.multiple_of(h * HD, 8), HD)


def query_of(qt, h, normed):
    start, off = window_of(h)
    win = pl.ds(start, WIN)
    row = lax.broadcasted_iota(jnp.int32, (WIN, 1), 0)
    mine = (row >= off) & (row < off + HD)
    own = qt[head_rows(h), :]
    if not normed:
        return jnp.where(mine, qt[win, :], 0.0).astype(BF)
    r = lax.rsqrt(jnp.sum(own * own, 0, keepdims=True) * (1.0 / HD) + 1e-6)
    return (jnp.where(mine, qt[win, :], 0.0) * r).astype(BF)


def softmax(s, shifted):
    if shifted:
        s = s - jnp.max(s, 0, keepdims=True)
    return jnp.exp2(s).astype(BF)


def values_of(vt, h, cols):
    v = vt[head_rows(h), cols].astype(BF)
    return jnp.concatenate([v, jnp.ones((8, v.shape[1]), BF)], 0)


def loop(n, body):
    def step(i, carry):
        body(i)
        return carry

    lax.fori_loop(0, n, step, 0)


def guarded(gain, run):
    bound = jnp.max(gain[...]) * HD

    @pl.when(bound <= SAFE)
    def _():
        run(False)

    @pl.when(bound > SAFE)
    def _():
        run(True)


def spatial_kernel(own, other, wqkv, wout, mod, gain, out, xin, k, qt, vt, at, *, rows):
    gather, spread = indicators()
    shift, scale, gate = mod[0:1, :], mod[1:2, :], mod[2:3, :]
    R = 256
    for b in range(rows // R):
        sl = pl.ds(b * R, R)
        xin[sl, :] = norm_rows(own[sl, :].astype(F32), shift, scale)
        xin[pl.ds(rows + b * R, R), :] = norm_rows(other[sl, :].astype(F32), shift, scale)
    for b in range(rows // R):
        sl = pl.ds(b * R, R)
        qt[:, sl] = dot(xin[sl, :], wqkv[:, 0:D]).T
    for b in range(2 * rows // R):
        sl = pl.ds(b * R, R)
        k[sl, :] = head_norm_rows(dot(xin[sl, :], wqkv[:, D:2 * D]), gather, spread, gain[...])
        vt[:, sl] = dot(xin[sl, :], wqkv[:, 2 * D:]).T

    def run(shifted):
        def pair(i):
            for h in (2 * i, 2 * i + 1):
                start, _ = window_of(h)
                q = query_of(qt, h, True)
                p = softmax(dot(k[:, pl.ds(start, WIN)], q), shifted)
                o = dot(values_of(vt, h, slice(None)), p)
                at[head_rows(h), :] = o[:HD] * (1.0 / o[HD:HD + 1])

        loop(HEADS // 2, pair)

    guarded(gain, run)
    for b in range(rows // R):
        sl = pl.ds(b * R, R)
        proj = dot(at[:, sl].T.astype(BF), wout[...])
        out[sl, :] = (own[sl, :].astype(F32) + gate * proj).astype(BF)


VMEM = pl.BlockSpec(memory_space=pltpu.VMEM)
PARAMS = pltpu.CompilerParams(vmem_limit_bytes=60 * 2**20)


def spatial(own, other, wqkv, wout, mod, gain):
    rows = own.shape[0]
    return pl.pallas_call(
        functools.partial(spatial_kernel, rows=rows),
        out_shape=jax.ShapeDtypeStruct((rows, D), BF),
        in_specs=[VMEM] * 6,
        out_specs=VMEM,
        scratch_shapes=[
            pltpu.VMEM((2 * rows, D), BF),
            pltpu.VMEM((2 * rows, D), BF),
            pltpu.VMEM((D, rows), F32),
            pltpu.VMEM((D, 2 * rows), F32),
            pltpu.VMEM((D, rows), F32),
        ],
        compiler_params=PARAMS,
        cost_estimate=pl.CostEstimate(flops=3 * 10**10, bytes_accessed=2 * 10**7, transcendentals=0),
        name="spatial",
    )(own, other, wqkv, wout, mod, gain)


def piece_copies(place, gathered, weight, sems):
    z = place[0]
    width = gathered.shape[3]
    parts = weight.shape[1] // width
    copies = []
    for x in range(4):
        for y in range(parts):
            for core in range(2):
                low, count = (0, HALF) if core == 0 else (HALF - 64, 64)
                for dz in range(2):
                    shard = 2 * x + (z if dz == 0 else 1 - z)
                    row = pl.multiple_of(shard * SHARD + core * HALF, 16)
                    dst = weight.at[pl.ds(row, count), pl.ds(y * width, width)]
                    src = gathered.at[(x * parts + y) * 2 + core, dz, pl.ds(low, count), :]
                    copies.append(pltpu.make_async_copy(src, dst, sems.at[len(copies)]))
    return copies


def ordered(rows, source_of):
    to = lax.broadcasted_iota(jnp.int32, (rows, rows), 0)
    source = lax.broadcasted_iota(jnp.int32, (rows, rows), 1)
    return (source == source_of(to)).astype(F32).astype(BF)


def temporal_kernel(place, gathered, x, valid, mod, gain, out, w, xp, xin, k, qt, vt, at, sems, *, rows, frames):
    copies = piece_copies(place, gathered, w, sems)
    for copy in copies:
        copy.start()
    gather, spread = indicators()
    places = rows // frames
    shift, scale, gate = mod[3:4, :], mod[4:5, :], mod[5:6, :]
    R = 256
    order = ordered(rows, lambda to: lax.rem(to, frames) * places + to // frames)
    for b in range(rows // R):
        sl = pl.ds(b * R, R)
        moved = dot(order[b * R:(b + 1) * R, :], x[...])
        xp[sl, :] = moved.astype(BF)
        xin[sl, :] = norm_rows(moved, shift, scale)
    for copy in copies:
        copy.wait()
    for b in range(rows // R):
        sl = pl.ds(b * R, R)
        qt[:, sl] = dot(xin[sl, :], w[:, 0:D]).T
        k[sl, :] = head_norm_rows(dot(xin[sl, :], w[:, D:2 * D]), gather, spread, gain[...])
        vt[:, sl] = dot(xin[sl, :], w[:, 2 * D:3 * D]).T

    key = lax.broadcasted_iota(jnp.int32, (R, R), 0) // frames
    query = lax.broadcasted_iota(jnp.int32, (R, R), 1) // frames
    bias = jnp.where(key == query, 0.0, -1e30) + valid[...]

    def run(shifted):
        def pair(i):
            for h in (2 * i, 2 * i + 1):
                start, _ = window_of(h)
                q = query_of(qt, h, True)
                for b in range(rows // R):
                    sl = pl.ds(b * R, R)
                    s = dot(k[sl, pl.ds(start, WIN)], q[:, b * R:(b + 1) * R]) + bias
                    o = dot(values_of(vt, h, sl), softmax(s, shifted))
                    at[head_rows(h), sl] = o[:HD] * (1.0 / o[HD:HD + 1])

        loop(HEADS // 2, pair)

    guarded(gain, run)
    for b in range(rows // R):
        sl = pl.ds(b * R, R)
        proj = dot(at[:, sl].T.astype(BF), w[:, 3 * D:])
        xin[sl, :] = (xp[sl, :].astype(F32) + gate * proj).astype(BF)
    groups = frames // 8

    def source_of(to):
        place, frame = lax.rem(to, places), to // places
        return place * frames + lax.rem(frame, 8) * groups + frame // 8

    order = ordered(rows, source_of)
    for b in range(rows // R):
        out[pl.ds(b * R, R), :] = dot(order[b * R:(b + 1) * R, :], xin[...]).astype(BF)


def temporal(place, gathered, x, valid, mod, gain):
    rows = x.shape[0]
    hbm = pl.BlockSpec(memory_space=pl.ANY)
    return pl.pallas_call(
        functools.partial(temporal_kernel, rows=rows, frames=64),
        out_shape=jax.ShapeDtypeStruct((rows, D), BF),
        in_specs=[pl.BlockSpec(memory_space=pltpu.SMEM)] + [hbm] + [VMEM] * 4,
        out_specs=VMEM,
        scratch_shapes=[
            pltpu.VMEM((D, 4 * D), BF),
            pltpu.VMEM((rows, D), BF),
            pltpu.VMEM((rows, D), BF),
            pltpu.VMEM((rows, D), BF),
            pltpu.VMEM((D, rows), F32),
            pltpu.VMEM((D, rows), F32),
            pltpu.VMEM((D, rows), F32),
            pltpu.SemaphoreType.DMA((64,)),
        ],
        compiler_params=PARAMS,
        cost_estimate=pl.CostEstimate(flops=2 * 10**10, bytes_accessed=2 * 10**7, transcendentals=0),
        name="temporal",
    )(place, gathered, x, valid, mod, gain)


def cross_kernel(place, gathered, x, tk, tvt, out, w, qt, at, sems):
    copies = piece_copies(place, gathered, w, sems)
    for copy in copies:
        copy.start()
    rows = x.shape[0]
    R = 256
    for copy in copies:
        copy.wait()
    for b in range(rows // R):
        sl = pl.ds(b * R, R)
        cq = dot(x[sl, :], w[:, :D]).astype(BF).astype(F32) * (HD ** -0.5 * 1.4426950408889634)
        qt[:, sl] = cq.T
    lane = lax.broadcasted_iota(jnp.int32, (8, TPAD), 1)
    ones = (lane < TEXT).astype(F32).astype(BF)

    def pair(i):
        for h in (2 * i, 2 * i + 1):
            start, _ = window_of(h)
            q = query_of(qt, h, False)
            p = softmax(dot(tk[:, pl.ds(start, WIN)], q), True)
            v = jnp.concatenate([tvt[head_rows(h), :].astype(BF), ones], 0)
            o = dot(v, p)
            at[head_rows(h), :] = o[:HD] * (1.0 / o[HD:HD + 1])

    loop(HEADS // 2, pair)
    for b in range(rows // R):
        sl = pl.ds(b * R, R)
        mixed = x[sl, :].astype(F32) + dot(at[:, sl].T.astype(BF), w[:, D:])
        for g in range(R // 64):
            for f in range(8):
                low = g * 64 + f * 8
                out[f, pl.ds((b * (R // 64) + g) * 8, 8), :] = mixed[low:low + 8, :].astype(BF)


def cross(place, gathered, x, tk, tvt):
    rows = x.shape[0]
    hbm = pl.BlockSpec(memory_space=pl.ANY)
    return pl.pallas_call(
        cross_kernel,
        out_shape=jax.ShapeDtypeStruct((8, rows // 8, D), BF),
        in_specs=[pl.BlockSpec(memory_space=pltpu.SMEM)] + [hbm] + [VMEM] * 3,
        out_specs=VMEM,
        scratch_shapes=[
            pltpu.VMEM((D, 2 * D), BF),
            pltpu.VMEM((D, rows), F32),
            pltpu.VMEM((D, rows), F32),
            pltpu.SemaphoreType.DMA((64,)),
        ],
        compiler_params=PARAMS,
        cost_estimate=pl.CostEstimate(flops=2 * 10**10, bytes_accessed=2 * 10**7, transcendentals=0),
        name="cross",
    )(place, gathered, x, tk, tvt)


import numpy as np
from jax.sharding import Mesh, PartitionSpec as P

XZ = ("x", "zh")
YZ = ("y", "zl")
RIGHT = [(i, (i + 1) % 4) for i in range(4)]
LEFT = [(i, (i + 3) % 4) for i in range(4)]
SWAP = [(0, 1), (1, 0)]
ACROSS = [(0, 3), (3, 0), (1, 2), (2, 1)]
bar = lax.optimization_barrier


def gains(gain_q, gain_k):
    return jnp.tile(gain_q * gain_k * (HD ** -0.5 * 1.4426950408889634), HEADS).reshape(1, D)


def across(v):
    return lax.ppermute(v, ("zh", "zl"), ACROSS)


def swap(v):
    return lax.ppermute(v, "c", SWAP)


def pos_quad(local, swapped):
    def both(v, axis, other):
        first = lax.axis_index(axis) == 0
        return jnp.concatenate([jnp.where(first, v, other), jnp.where(first, other, v)], 1)

    pair = both(local, "c", swapped)
    return both(pair, "zl", lax.ppermute(pair, "zl", SWAP))


def along_y(quad):
    return quad, lax.ppermute(quad, "y", RIGHT), lax.ppermute(quad, "y", [(i, (i + 2) % 4) for i in range(4)]), lax.ppermute(quad, "y", LEFT)


def in_order(steps):
    y = lax.axis_index("y")
    steps = jnp.stack(steps)
    return jnp.concatenate([lax.dynamic_index_in_dim(steps, lax.rem(y - i + 4, 4), 0, keepdims=False) for i in range(4)], 1)


def per_device(tokens, frame_valid, text, modulation, qk_gains, spatial_qkv, spatial_out, block_weights, cross_kv):
    core, y = lax.axis_index("c"), lax.axis_index("y")
    local = jnp.dot(text, cross_kv.reshape(D, 2 * HD), preferred_element_type=F32).astype(BF)
    swapped = swap(local)
    own = lax.all_to_all(tokens, YZ, 0, 0, tiled=True).reshape(-1, D)
    w1 = lax.dynamic_slice(block_weights, (64 * core, D * y), (HALF, D))
    w1, swapped = bar((w1, swapped))
    z1 = across(w1)
    both1 = jnp.stack([w1, z1])
    w2 = lax.dynamic_slice(block_weights, (64 * core, 4 * D), (HALF, 2 * D))
    w2, both1 = bar((w2, both1))
    gathered1 = lax.all_gather(both1, ("x", "y", "c"), axis=0)
    both2 = jnp.stack([w2, across(w2)])
    quad = pos_quad(local, swapped)
    gain_s = gains(qk_gains[0], qk_gains[1])
    gain_t = gains(qk_gains[2], qk_gains[3])
    seen = jnp.where(frame_valid.reshape(8, 8).T.reshape(64) > 0, 0.0, -1e30)
    valid = jnp.tile(seen, 4).reshape(256, 1).astype(F32)
    place = jnp.stack([lax.axis_index("zh"), core]).astype(jnp.int32)
    own, both2, quad, gain_s, gain_t, valid, place = bar((own, both2, quad, gain_s, gain_t, valid, place))

    other = swap(own)
    steps = along_y(quad)
    after_spatial = spatial(own, other, spatial_qkv, spatial_out, modulation, gain_s)
    after_spatial, steps = bar((after_spatial, steps))

    rows = lax.all_to_all(after_spatial.reshape(64, 8, D), YZ + XZ, 0, 0, tiled=True).reshape(-1, D)
    every = in_order(steps).reshape(TEXT, HEADS, 2, HD)
    tk = jnp.pad(every[:, :, 0].reshape(TEXT, D), ((0, TPAD - TEXT), (0, 0)), mode="edge")
    tvt = jnp.pad(every[:, :, 1].reshape(TEXT, D).T, ((0, 0), (0, TPAD - TEXT))).astype(F32)
    _, both2 = bar((rows, both2))
    gathered2 = lax.all_gather(both2, ("x", "c"), axis=0)
    after_temporal = temporal(place, gathered1, rows, valid, modulation, gain_t)

    back = lax.all_to_all(after_temporal.reshape(8, 64, D), XZ, 0, 0, tiled=True).reshape(-1, D)
    return cross(place, gathered2, back, tk, tvt)


def solution(mesh):
    fine = Mesh(np.asarray(mesh.devices).reshape(4, 2, 4, 2, 2), ("x", "zh", "y", "zl", "c"))
    pos = ("y", "zl", "c")
    placed = (P(XZ, pos, None), P(), P(), P(), P(), P(), P(XZ, None), P(None, None, pos))
    placed = placed[:6] + (P(),) + placed[6:]
    return jax.shard_map(per_device, mesh=fine, in_specs=placed, out_specs=P(XZ, pos, None), check_vma=False)
```

```python
import functools
import jax
import jax.numpy as jnp
from jax import lax
from jax.experimental import pallas as pl
from jax.experimental.pallas import tpu as pltpu

D = 1152
HD = 72
HEADS = 16
WIN = 256
TEXT = 300
TPAD = 304
SHARD = 144
HALF = 80
SAFE = 96.0
BF = jnp.bfloat16
F32 = jnp.float32


def dot(a, b):
    return jnp.dot(a, b, preferred_element_type=F32)


def indicators():
    feature = lax.broadcasted_iota(jnp.int32, (D, 128), 0)
    low = lax.broadcasted_iota(jnp.int32, (D, 128), 1) * HD
    gather = ((feature >= low) & (feature < low + HD)).astype(F32).astype(BF)
    feature = lax.broadcasted_iota(jnp.int32, (256, D), 1)
    low = lax.rem(lax.broadcasted_iota(jnp.int32, (256, D), 0), 128) * HD
    spread = ((feature >= low) & (feature < low + HD)).astype(F32).astype(BF)
    return gather, spread


def norm_rows(x, shift, scale):
    mean = jnp.mean(x, -1, keepdims=True)
    centred = x - mean
    r = lax.rsqrt(jnp.mean(centred * centred, -1, keepdims=True) + 1e-6)
    return (centred * r * (1.0 + scale) + shift).astype(BF)


def head_norm_rows(u, gather, spread, gain):
    total = dot((u * u).astype(BF), gather)
    r = lax.rsqrt(total * (1.0 / HD) + 1e-6)
    high = r.astype(BF)
    low = (r - high.astype(F32)).astype(BF)
    return (u * dot(jnp.concatenate([high, low], -1), spread) * gain).astype(BF)


def window_of(h):
    start = jnp.minimum((h * HD) // 128 * 128, D - WIN)
    return pl.multiple_of(start, 128), h * HD - start


def head_rows(h):
    return pl.ds(pl.multiple_of(h * HD, 8), HD)


def query_of(qt, h, normed):
    start, off = window_of(h)
    win = pl.ds(start, WIN)
    row = lax.broadcasted_iota(jnp.int32, (WIN, 1), 0)
    mine = (row >= off) & (row < off + HD)
    own = qt[head_rows(h), :]
    if not normed:
        return jnp.where(mine, qt[win, :], 0.0).astype(BF)
    r = lax.rsqrt(jnp.sum(own * own, 0, keepdims=True) * (1.0 / HD) + 1e-6)
    return (jnp.where(mine, qt[win, :], 0.0) * r).astype(BF)


def softmax(s, shifted):
    if shifted:
        s = s - jnp.max(s, 0, keepdims=True)
    return jnp.exp2(s).astype(BF)


def values_of(vt, h, cols):
    v = vt[head_rows(h), cols].astype(BF)
    return jnp.concatenate([v, jnp.ones((8, v.shape[1]), BF)], 0)


def loop(n, body):
    def step(i, carry):
        body(i)
        return carry

    lax.fori_loop(0, n, step, 0)


def guarded(gain, run):
    bound = jnp.max(gain[...]) * HD

    @pl.when(bound <= SAFE)
    def _():
        run(False)

    @pl.when(bound > SAFE)
    def _():
        run(True)


def spatial_kernel(own_hbm, other_hbm, wqkv_hbm, wout_hbm, mod, gain, out, own, other, wqkv, wout, xin, k, qt, vt, at, sems, *, rows):
    copies = [pltpu.make_async_copy(own_hbm, own, sems.at[0]), pltpu.make_async_copy(other_hbm, other, sems.at[1])]
    for i in range(3):
        columns = pl.ds(D * i, D)
        copies.append(pltpu.make_async_copy(wqkv_hbm.at[:, columns], wqkv.at[:, columns], sems.at[2 + i]))
    copies.append(pltpu.make_async_copy(wout_hbm, wout, sems.at[5]))
    for copy in copies:
        copy.start()
    gather, spread = indicators()
    shift, scale, gate = mod[0:1, :], mod[1:2, :], mod[2:3, :]
    R = 256

    def block(i):
        return pl.ds(pl.multiple_of(i * R, R), R)

    def normed(i):
        sl, far = block(i), block(i + rows // R)
        xin[sl, :] = norm_rows(own[sl, :].astype(F32), shift, scale)
        xin[far, :] = norm_rows(other[sl, :].astype(F32), shift, scale)

    def project(i):
        sl, far = block(i), block(i + rows // R)
        qt[:, sl] = dot(xin[sl, :], wqkv[:, 0:D]).T
        for to in (sl, far):
            k[to, :] = head_norm_rows(dot(xin[to, :], wqkv[:, D:2 * D]), gather, spread, gain[...])
            vt[:, to] = dot(xin[to, :], wqkv[:, 2 * D:]).T

    for copy in copies[:2]:
        copy.wait()
    loop(rows // R, normed)
    for copy in copies[2:5]:
        copy.wait()
    loop(rows // R, project)

    def run(shifted):
        def pair(i):
            for h in (2 * i, 2 * i + 1):
                start, _ = window_of(h)
                q = query_of(qt, h, True)
                p = softmax(dot(k[:, pl.ds(start, WIN)], q), shifted)
                o = dot(values_of(vt, h, slice(None)), p)
                at[head_rows(h), :] = o[:HD] * (1.0 / o[HD:HD + 1])

        loop(HEADS // 2, pair)

    guarded(gain, run)

    def finish(i):
        sl = block(i)
        proj = dot(at[:, sl].T.astype(BF), wout[...])
        out[sl, :] = (own[sl, :].astype(F32) + gate * proj).astype(BF)

    copies[5].wait()
    loop(rows // R, finish)


VMEM = pl.BlockSpec(memory_space=pltpu.VMEM)
HBM = pl.BlockSpec(memory_space=pl.ANY)
PARAMS = pltpu.CompilerParams(vmem_limit_bytes=60 * 2**20)


def spatial(own, other, wqkv, wout, mod, gain):
    rows = own.shape[0]
    return pl.pallas_call(
        functools.partial(spatial_kernel, rows=rows),
        out_shape=jax.ShapeDtypeStruct((rows, D), BF),
        in_specs=[HBM] * 4 + [VMEM] * 2,
        out_specs=VMEM,
        scratch_shapes=[
            pltpu.VMEM((rows, D), BF),
            pltpu.VMEM((rows, D), BF),
            pltpu.VMEM((D, 3 * D), BF),
            pltpu.VMEM((D, D), BF),
            pltpu.VMEM((2 * rows, D), BF),
            pltpu.VMEM((2 * rows, D), BF),
            pltpu.VMEM((D, rows), F32),
            pltpu.VMEM((D, 2 * rows), F32),
            pltpu.VMEM((D, rows), F32),
            pltpu.SemaphoreType.DMA((6,)),
        ],
        compiler_params=PARAMS,
        cost_estimate=pl.CostEstimate(flops=3 * 10**10, bytes_accessed=2 * 10**7, transcendentals=0),
        name="spatial",
    )(own, other, wqkv, wout, mod, gain)


def piece_copies(place, gathered, weight, sems):
    z = place[0]
    width = gathered.shape[3]
    parts = weight.shape[1] // width
    copies = []
    for y in range(parts):
        for x in range(4):
            for core in range(2):
                low, count = (0, HALF) if core == 0 else (HALF - 64, 64)
                for dz in range(2):
                    shard = 2 * x + (z if dz == 0 else 1 - z)
                    row = pl.multiple_of(shard * SHARD + core * HALF, 16)
                    dst = weight.at[pl.ds(row, count), pl.ds(y * width, width)]
                    src = gathered.at[(x * parts + y) * 2 + core, dz, pl.ds(low, count), :]
                    copies.append(pltpu.make_async_copy(src, dst, sems.at[len(copies)]))
    return copies


def ordered(rows, source_of):
    to = lax.broadcasted_iota(jnp.int32, (rows, rows), 0)
    source = lax.broadcasted_iota(jnp.int32, (rows, rows), 1)
    return (source == source_of(to)).astype(F32).astype(BF)


def temporal_kernel(place, gathered, x, mod, gain, out, w, xp, xin, k, qt, vt, at, sems, *, rows, frames):
    copies = piece_copies(place, gathered, w, sems)
    for copy in copies:
        copy.start()
    gather, spread = indicators()
    places = rows // frames
    shift, scale, gate = mod[3:4, :], mod[4:5, :], mod[5:6, :]
    R = 256
    order = ordered(rows, lambda to: lax.rem(to, frames) * places + to // frames)
    for b in range(rows // R):
        sl = pl.ds(b * R, R)
        moved = dot(order[b * R:(b + 1) * R, :], x[...])
        xp[sl, :] = moved.astype(BF)
        xin[sl, :] = norm_rows(moved, shift, scale)
    for copy in copies[:48]:
        copy.wait()
    for b in range(rows // R):
        sl = pl.ds(b * R, R)
        qt[:, sl] = dot(xin[sl, :], w[:, 0:D]).T
        k[sl, :] = head_norm_rows(dot(xin[sl, :], w[:, D:2 * D]), gather, spread, gain[...])
        vt[:, sl] = dot(xin[sl, :], w[:, 2 * D:3 * D]).T

    row = lax.broadcasted_iota(jnp.int32, (R, R), 0)
    held = lax.rem(row, frames)
    frame = lax.rem(held, frames // 8) * 8 + held // (frames // 8)
    query = lax.broadcasted_iota(jnp.int32, (R, R), 1) // frames
    bias = jnp.where((row // frames == query) & (frame < place[2]), 0.0, -1e30)

    def run(shifted):
        def pair(i):
            for h in (2 * i, 2 * i + 1):
                start, _ = window_of(h)
                q = query_of(qt, h, True)
                for b in range(rows // R):
                    sl = pl.ds(b * R, R)
                    s = dot(k[sl, pl.ds(start, WIN)], q[:, b * R:(b + 1) * R]) + bias
                    o = dot(values_of(vt, h, sl), softmax(s, shifted))
                    at[head_rows(h), sl] = o[:HD] * (1.0 / o[HD:HD + 1])

        loop(HEADS // 2, pair)

    guarded(gain, run)
    for copy in copies[48:]:
        copy.wait()
    for b in range(rows // R):
        sl = pl.ds(b * R, R)
        proj = dot(at[:, sl].T.astype(BF), w[:, 3 * D:])
        xin[sl, :] = (xp[sl, :].astype(F32) + gate * proj).astype(BF)
    groups = frames // 8

    def source_of(to):
        place, frame = lax.rem(to, places), to // places
        return place * frames + lax.rem(frame, 8) * groups + frame // 8

    order = ordered(rows, source_of)
    for b in range(rows // R):
        out[pl.ds(b * R, R), :] = dot(order[b * R:(b + 1) * R, :], xin[...]).astype(BF)


def temporal(place, gathered, x, mod, gain):
    rows = x.shape[0]
    return pl.pallas_call(
        functools.partial(temporal_kernel, rows=rows, frames=64),
        out_shape=jax.ShapeDtypeStruct((rows, D), BF),
        in_specs=[pl.BlockSpec(memory_space=pltpu.SMEM)] + [HBM] + [VMEM] * 3,
        out_specs=VMEM,
        scratch_shapes=[
            pltpu.VMEM((D, 4 * D), BF),
            pltpu.VMEM((rows, D), BF),
            pltpu.VMEM((rows, D), BF),
            pltpu.VMEM((rows, D), BF),
            pltpu.VMEM((D, rows), F32),
            pltpu.VMEM((D, rows), F32),
            pltpu.VMEM((D, rows), F32),
            pltpu.SemaphoreType.DMA((64,)),
        ],
        compiler_params=PARAMS,
        cost_estimate=pl.CostEstimate(flops=2 * 10**10, bytes_accessed=2 * 10**7, transcendentals=0),
        name="temporal",
    )(place, gathered, x, mod, gain)


def cross_kernel(place, gathered, x, tk, tvt, out, w, qt, at, sems):
    copies = piece_copies(place, gathered, w, sems)
    for copy in copies:
        copy.start()
    rows = x.shape[0]
    R = 256
    for copy in copies:
        copy.wait()
    for b in range(rows // R):
        sl = pl.ds(b * R, R)
        cq = dot(x[sl, :], w[:, :D]).astype(BF).astype(F32) * (HD ** -0.5 * 1.4426950408889634)
        qt[:, sl] = cq.T
    lane = lax.broadcasted_iota(jnp.int32, (8, TPAD), 1)
    ones = (lane < TEXT).astype(F32).astype(BF)

    def pair(i):
        for h in (2 * i, 2 * i + 1):
            start, _ = window_of(h)
            q = query_of(qt, h, False)
            p = softmax(dot(tk[:, pl.ds(start, WIN)], q), True)
            v = jnp.concatenate([tvt[head_rows(h), :].astype(BF), ones], 0)
            o = dot(v, p)
            at[head_rows(h), :] = o[:HD] * (1.0 / o[HD:HD + 1])

    loop(HEADS // 2, pair)
    for b in range(rows // R):
        sl = pl.ds(b * R, R)
        mixed = x[sl, :].astype(F32) + dot(at[:, sl].T.astype(BF), w[:, D:])
        for g in range(R // 64):
            for f in range(8):
                low = g * 64 + f * 8
                out[f, pl.ds((b * (R // 64) + g) * 8, 8), :] = mixed[low:low + 8, :].astype(BF)


def cross(place, gathered, x, tk, tvt):
    rows = x.shape[0]
    return pl.pallas_call(
        cross_kernel,
        out_shape=jax.ShapeDtypeStruct((8, rows // 8, D), BF),
        in_specs=[pl.BlockSpec(memory_space=pltpu.SMEM)] + [HBM] + [VMEM] * 3,
        out_specs=VMEM,
        scratch_shapes=[
            pltpu.VMEM((D, 2 * D), BF),
            pltpu.VMEM((D, rows), F32),
            pltpu.VMEM((D, rows), F32),
            pltpu.SemaphoreType.DMA((64,)),
        ],
        compiler_params=PARAMS,
        cost_estimate=pl.CostEstimate(flops=2 * 10**10, bytes_accessed=2 * 10**7, transcendentals=0),
        name="cross",
    )(place, gathered, x, tk, tvt)


import numpy as np
from jax.sharding import Mesh, PartitionSpec as P

XZ = ("x", "zh")
YZ = ("y", "zl")
RIGHT = [(i, (i + 1) % 4) for i in range(4)]
LEFT = [(i, (i + 3) % 4) for i in range(4)]
SWAP = [(0, 1), (1, 0)]
ACROSS = [(0, 3), (3, 0), (1, 2), (2, 1)]
bar = lax.optimization_barrier


def gains(gain_q, gain_k):
    return jnp.tile(gain_q * gain_k * (HD ** -0.5 * 1.4426950408889634), HEADS).reshape(1, D)


def across(v):
    return lax.ppermute(v, ("zh", "zl"), ACROSS)


def swap(v):
    return lax.ppermute(v, "c", SWAP)


def in_pairs(v, axis, other):
    first = lax.axis_index(axis) == 0
    return jnp.concatenate([jnp.where(first, v, other), jnp.where(first, other, v)], 1)


def along_y(quad):
    return quad, lax.ppermute(quad, "y", RIGHT), lax.ppermute(quad, "y", [(i, (i + 2) % 4) for i in range(4)]), lax.ppermute(quad, "y", LEFT)


def in_order(steps):
    y = lax.axis_index("y")
    steps = jnp.stack(steps)
    return jnp.concatenate([lax.dynamic_index_in_dim(steps, lax.rem(y - i + 4, 4), 0, keepdims=False) for i in range(4)], 1)


def per_device(tokens, frame_valid, text, modulation, qk_gains, spatial_qkv, spatial_out, block_weights, cross_kv):
    core, y = lax.axis_index("c"), lax.axis_index("y")
    own = lax.all_to_all(tokens, YZ, 0, 0, tiled=True).reshape(-1, D)
    w1 = lax.dynamic_slice(block_weights, (64 * core, D * y), (HALF, D))
    w2 = lax.dynamic_slice(block_weights, (64 * core, 4 * D), (HALF, 2 * D))
    both1 = jnp.stack([w1, across(w1)])
    local = jnp.dot(text, cross_kv.reshape(D, 2 * HD), preferred_element_type=F32).astype(BF)
    gain_s = gains(qk_gains[0], qk_gains[1])
    gain_t = gains(qk_gains[2], qk_gains[3])
    count = jnp.sum((frame_valid > 0).astype(jnp.int32))
    place = jnp.stack([lax.axis_index("zh"), core, count]).astype(jnp.int32)
    both1, local, gain_s, gain_t, place = bar((both1, local, gain_s, gain_t, place))
    gathered1 = lax.all_gather(both1, ("x", "y", "c"), axis=0)
    own, local, w2 = bar((own, local, w2))

    other = swap(own)
    swapped = swap(local)
    z2 = across(w2)
    after_spatial = spatial(own, other, spatial_qkv, spatial_out, modulation, gain_s)
    after_spatial, swapped, z2 = bar((after_spatial, swapped, z2))

    rows = lax.all_to_all(after_spatial.reshape(64, 8, D), YZ + XZ, 0, 0, tiled=True).reshape(-1, D)
    pair = in_pairs(local, "c", swapped)
    besides = lax.ppermute(pair, "zl", SWAP)
    rows, besides = bar((rows, besides))
    steps = along_y(in_pairs(pair, "zl", besides))
    _, both2 = bar((rows, jnp.stack([w2, z2])))
    gathered2 = lax.all_gather(both2, ("x", "c"), axis=0)
    after_temporal = temporal(place, gathered1, rows, modulation, gain_t)
    after_temporal, steps = bar((after_temporal, steps))

    every = in_order(steps).reshape(TEXT, HEADS, 2, HD)
    tk = jnp.pad(every[:, :, 0].reshape(TEXT, D), ((0, TPAD - TEXT), (0, 0)), mode="edge")
    tvt = jnp.pad(every[:, :, 1].reshape(TEXT, D).T, ((0, 0), (0, TPAD - TEXT))).astype(F32)
    back = lax.all_to_all(after_temporal.reshape(8, 64, D), XZ, 0, 0, tiled=True).reshape(-1, D)
    return cross(place, gathered2, back, tk, tvt)


def solution(mesh):
    fine = Mesh(np.asarray(mesh.devices).reshape(4, 2, 4, 2, 2), ("x", "zh", "y", "zl", "c"))
    pos = ("y", "zl", "c")
    placed = (P(XZ, pos, None), P(), P(), P(), P(), P(), P(XZ, None), P(None, None, pos))
    placed = placed[:6] + (P(),) + placed[6:]
    return jax.shard_map(per_device, mesh=fine, in_specs=placed, out_specs=P(XZ, pos, None), check_vma=False)
```

```python
import functools
import jax
import jax.numpy as jnp
from jax import lax
from jax.experimental import pallas as pl
from jax.experimental.pallas import tpu as pltpu

D = 1152
HD = 72
HEADS = 16
WIN = 256
TEXT = 300
TPAD = 304
SHARD = 144
HALF = 80
SAFE = 96.0
BF = jnp.bfloat16
F32 = jnp.float32


def dot(a, b):
    return jnp.dot(a, b, preferred_element_type=F32)


def indicators():
    feature = lax.broadcasted_iota(jnp.int32, (D, 128), 0)
    low = lax.broadcasted_iota(jnp.int32, (D, 128), 1) * HD
    gather = ((feature >= low) & (feature < low + HD)).astype(F32).astype(BF)
    feature = lax.broadcasted_iota(jnp.int32, (256, D), 1)
    low = lax.rem(lax.broadcasted_iota(jnp.int32, (256, D), 0), 128) * HD
    spread = ((feature >= low) & (feature < low + HD)).astype(F32).astype(BF)
    return gather, spread


def norm_rows(x, shift, scale):
    mean = jnp.mean(x, -1, keepdims=True)
    centred = x - mean
    r = lax.rsqrt(jnp.mean(centred * centred, -1, keepdims=True) + 1e-6)
    return (centred * r * (1.0 + scale) + shift).astype(BF)


def head_norm_rows(u, gather, spread, gain):
    total = dot((u * u).astype(BF), gather)
    r = lax.rsqrt(total * (1.0 / HD) + 1e-6)
    high = r.astype(BF)
    low = (r - high.astype(F32)).astype(BF)
    return (u * dot(jnp.concatenate([high, low], -1), spread) * gain).astype(BF)


def window_of(h):
    start = jnp.minimum((h * HD) // 128 * 128, D - WIN)
    return pl.multiple_of(start, 128), h * HD - start


def head_rows(h):
    return pl.ds(pl.multiple_of(h * HD, 8), HD)


def query_of(qt, h, normed):
    start, off = window_of(h)
    win = pl.ds(start, WIN)
    row = lax.broadcasted_iota(jnp.int32, (WIN, 1), 0)
    mine = (row >= off) & (row < off + HD)
    own = qt[head_rows(h), :]
    if not normed:
        return jnp.where(mine, qt[win, :], 0.0).astype(BF)
    r = lax.rsqrt(jnp.sum(own * own, 0, keepdims=True) * (1.0 / HD) + 1e-6)
    return (jnp.where(mine, qt[win, :], 0.0) * r).astype(BF)


def softmax(s, shifted):
    if shifted:
        s = s - jnp.max(s, 0, keepdims=True)
    return jnp.exp2(s).astype(BF)


def values_of(vt, h, cols):
    v = vt[head_rows(h), cols].astype(BF)
    return jnp.concatenate([v, jnp.ones((8, v.shape[1]), BF)], 0)


def loop(n, body):
    def step(i, carry):
        body(i)
        return carry

    lax.fori_loop(0, n, step, 0)


def guarded(gain, run):
    bound = jnp.max(gain[...]) * HD

    @pl.when(bound <= SAFE)
    def _():
        run(False)

    @pl.when(bound > SAFE)
    def _():
        run(True)


def spatial_kernel(own_hbm, other_hbm, wqkv_hbm, wout_hbm, mod, gain, out, own, other, wqkv, wout, xin, k, qt, vt, at, sems, *, rows):
    copies = [pltpu.make_async_copy(own_hbm, own, sems.at[0]), pltpu.make_async_copy(other_hbm, other, sems.at[1])]
    for i in range(3):
        columns = pl.ds(D * i, D)
        copies.append(pltpu.make_async_copy(wqkv_hbm.at[:, columns], wqkv.at[:, columns], sems.at[2 + i]))
    copies.append(pltpu.make_async_copy(wout_hbm, wout, sems.at[5]))
    for copy in copies:
        copy.start()
    gather, spread = indicators()
    shift, scale, gate = mod[0:1, :], mod[1:2, :], mod[2:3, :]
    R = 256

    def block(i):
        return pl.ds(pl.multiple_of(i * R, R), R)

    def normed(i):
        sl, far = block(i), block(i + rows // R)
        xin[sl, :] = norm_rows(own[sl, :].astype(F32), shift, scale)
        xin[far, :] = norm_rows(other[sl, :].astype(F32), shift, scale)

    def project(i):
        sl, far = block(i), block(i + rows // R)
        qt[:, sl] = dot(xin[sl, :], wqkv[:, 0:D]).T
        for to in (sl, far):
            k[to, :] = head_norm_rows(dot(xin[to, :], wqkv[:, D:2 * D]), gather, spread, gain[...])
            vt[:, to] = dot(xin[to, :], wqkv[:, 2 * D:]).T

    for copy in copies[:2]:
        copy.wait()
    loop(rows // R, normed)
    for copy in copies[2:5]:
        copy.wait()
    loop(rows // R, project)

    def run(shifted):
        def pair(i):
            for h in (2 * i, 2 * i + 1):
                start, _ = window_of(h)
                q = query_of(qt, h, True)
                p = softmax(dot(k[:, pl.ds(start, WIN)], q), shifted)
                o = dot(values_of(vt, h, slice(None)), p)
                at[head_rows(h), :] = o[:HD] * (1.0 / o[HD:HD + 1])

        loop(HEADS // 2, pair)

    guarded(gain, run)

    def finish(i):
        sl = block(i)
        proj = dot(at[:, sl].T.astype(BF), wout[...])
        out[sl, :] = (own[sl, :].astype(F32) + gate * proj).astype(BF)

    copies[5].wait()
    loop(rows // R, finish)


VMEM = pl.BlockSpec(memory_space=pltpu.VMEM)
HBM = pl.BlockSpec(memory_space=pl.ANY)
PARAMS = pltpu.CompilerParams(vmem_limit_bytes=60 * 2**20)


def spatial(own, other, wqkv, wout, mod, gain):
    rows = own.shape[0]
    return pl.pallas_call(
        functools.partial(spatial_kernel, rows=rows),
        out_shape=jax.ShapeDtypeStruct((rows, D), BF),
        in_specs=[HBM] * 4 + [VMEM] * 2,
        out_specs=VMEM,
        scratch_shapes=[
            pltpu.VMEM((rows, D), BF),
            pltpu.VMEM((rows, D), BF),
            pltpu.VMEM((D, 3 * D), BF),
            pltpu.VMEM((D, D), BF),
            pltpu.VMEM((2 * rows, D), BF),
            pltpu.VMEM((2 * rows, D), BF),
            pltpu.VMEM((D, rows), F32),
            pltpu.VMEM((D, 2 * rows), F32),
            pltpu.VMEM((D, rows), F32),
            pltpu.SemaphoreType.DMA((6,)),
        ],
        compiler_params=PARAMS,
        cost_estimate=pl.CostEstimate(flops=3 * 10**10, bytes_accessed=2 * 10**7, transcendentals=0),
        name="spatial",
    )(own, other, wqkv, wout, mod, gain)


def piece_copies(place, gathered, weight, sems):
    z = place[0]
    parts = weight.shape[1] // gathered.shape[3]
    copies = []
    for column in range(0, weight.shape[1], D):
        y, at = divmod(column, gathered.shape[3])
        for x in range(4):
            for core in range(2):
                low, count = (0, HALF) if core == 0 else (HALF - 64, 64)
                for dz in range(2):
                    shard = 2 * x + (z if dz == 0 else 1 - z)
                    row = pl.multiple_of(shard * SHARD + core * HALF, 16)
                    dst = weight.at[pl.ds(row, count), pl.ds(column, D)]
                    src = gathered.at[(x * parts + y) * 2 + core, dz, pl.ds(low, count), pl.ds(at, D)]
                    copies.append(pltpu.make_async_copy(src, dst, sems.at[len(copies)]))
    return copies


def ordered(rows, source_of):
    to = lax.broadcasted_iota(jnp.int32, (rows, rows), 0)
    source = lax.broadcasted_iota(jnp.int32, (rows, rows), 1)
    return (source == source_of(to)).astype(F32).astype(BF)


def temporal_kernel(place, gathered, x, mod, gain, out, w, xp, xin, k, qt, vt, at, sems, *, rows, frames):
    copies = piece_copies(place, gathered, w, sems)
    for copy in copies:
        copy.start()
    gather, spread = indicators()
    places = rows // frames
    shift, scale, gate = mod[3:4, :], mod[4:5, :], mod[5:6, :]
    R = 256
    order = ordered(rows, lambda to: lax.rem(to, frames) * places + to // frames)
    for b in range(rows // R):
        sl = pl.ds(b * R, R)
        moved = dot(order[b * R:(b + 1) * R, :], x[...])
        xp[sl, :] = moved.astype(BF)
        xin[sl, :] = norm_rows(moved, shift, scale)
    for copy in copies[:48]:
        copy.wait()
    for b in range(rows // R):
        sl = pl.ds(b * R, R)
        qt[:, sl] = dot(xin[sl, :], w[:, 0:D]).T
        k[sl, :] = head_norm_rows(dot(xin[sl, :], w[:, D:2 * D]), gather, spread, gain[...])
        vt[:, sl] = dot(xin[sl, :], w[:, 2 * D:3 * D]).T

    row = lax.broadcasted_iota(jnp.int32, (R, R), 0)
    held = lax.rem(row, frames)
    frame = lax.rem(held, frames // 8) * 8 + held // (frames // 8)
    query = lax.broadcasted_iota(jnp.int32, (R, R), 1) // frames
    bias = jnp.where((row // frames == query) & (frame < place[2]), 0.0, -1e30)

    def run(shifted):
        def pair(i):
            for h in (2 * i, 2 * i + 1):
                start, _ = window_of(h)
                q = query_of(qt, h, True)
                for b in range(rows // R):
                    sl = pl.ds(b * R, R)
                    s = dot(k[sl, pl.ds(start, WIN)], q[:, b * R:(b + 1) * R]) + bias
                    o = dot(values_of(vt, h, sl), softmax(s, shifted))
                    at[head_rows(h), sl] = o[:HD] * (1.0 / o[HD:HD + 1])

        loop(HEADS // 2, pair)

    guarded(gain, run)
    for copy in copies[48:]:
        copy.wait()
    for b in range(rows // R):
        sl = pl.ds(b * R, R)
        proj = dot(at[:, sl].T.astype(BF), w[:, 3 * D:])
        xin[sl, :] = (xp[sl, :].astype(F32) + gate * proj).astype(BF)
    groups = frames // 8

    def source_of(to):
        place, frame = lax.rem(to, places), to // places
        return place * frames + lax.rem(frame, 8) * groups + frame // 8

    order = ordered(rows, source_of)
    for b in range(rows // R):
        out[pl.ds(b * R, R), :] = dot(order[b * R:(b + 1) * R, :], xin[...]).astype(BF)


def temporal(place, gathered, x, mod, gain):
    rows = x.shape[0]
    return pl.pallas_call(
        functools.partial(temporal_kernel, rows=rows, frames=64),
        out_shape=jax.ShapeDtypeStruct((rows, D), BF),
        in_specs=[pl.BlockSpec(memory_space=pltpu.SMEM)] + [HBM] + [VMEM] * 3,
        out_specs=VMEM,
        scratch_shapes=[
            pltpu.VMEM((D, 4 * D), BF),
            pltpu.VMEM((rows, D), BF),
            pltpu.VMEM((rows, D), BF),
            pltpu.VMEM((rows, D), BF),
            pltpu.VMEM((D, rows), F32),
            pltpu.VMEM((D, rows), F32),
            pltpu.VMEM((D, rows), F32),
            pltpu.SemaphoreType.DMA((64,)),
        ],
        compiler_params=PARAMS,
        cost_estimate=pl.CostEstimate(flops=2 * 10**10, bytes_accessed=2 * 10**7, transcendentals=0),
        name="temporal",
    )(place, gathered, x, mod, gain)


def cross_kernel(place, gathered, x, tk, tvt, out, w, qt, at, sems):
    copies = piece_copies(place, gathered, w, sems)
    for copy in copies:
        copy.start()
    rows = x.shape[0]
    R = 256
    for copy in copies[:16]:
        copy.wait()
    for b in range(rows // R):
        sl = pl.ds(b * R, R)
        cq = dot(x[sl, :], w[:, :D]).astype(BF).astype(F32) * (HD ** -0.5 * 1.4426950408889634)
        qt[:, sl] = cq.T
    lane = lax.broadcasted_iota(jnp.int32, (8, TPAD), 1)
    ones = (lane < TEXT).astype(F32).astype(BF)

    def pair(i):
        for h in (2 * i, 2 * i + 1):
            start, _ = window_of(h)
            q = query_of(qt, h, False)
            p = softmax(dot(tk[:, pl.ds(start, WIN)], q), True)
            v = jnp.concatenate([tvt[head_rows(h), :].astype(BF), ones], 0)
            o = dot(v, p)
            at[head_rows(h), :] = o[:HD] * (1.0 / o[HD:HD + 1])

    loop(HEADS // 2, pair)
    for copy in copies[16:]:
        copy.wait()
    for b in range(rows // R):
        sl = pl.ds(b * R, R)
        mixed = x[sl, :].astype(F32) + dot(at[:, sl].T.astype(BF), w[:, D:])
        for g in range(R // 64):
            for f in range(8):
                low = g * 64 + f * 8
                out[f, pl.ds((b * (R // 64) + g) * 8, 8), :] = mixed[low:low + 8, :].astype(BF)


def cross(place, gathered, x, tk, tvt):
    rows = x.shape[0]
    return pl.pallas_call(
        cross_kernel,
        out_shape=jax.ShapeDtypeStruct((8, rows // 8, D), BF),
        in_specs=[pl.BlockSpec(memory_space=pltpu.SMEM)] + [HBM] + [VMEM] * 3,
        out_specs=VMEM,
        scratch_shapes=[
            pltpu.VMEM((D, 2 * D), BF),
            pltpu.VMEM((D, rows), F32),
            pltpu.VMEM((D, rows), F32),
            pltpu.SemaphoreType.DMA((64,)),
        ],
        compiler_params=PARAMS,
        cost_estimate=pl.CostEstimate(flops=2 * 10**10, bytes_accessed=2 * 10**7, transcendentals=0),
        name="cross",
    )(place, gathered, x, tk, tvt)


import numpy as np
from jax.sharding import Mesh, PartitionSpec as P

XZ = ("x", "zh")
YZ = ("y", "zl")
RIGHT = [(i, (i + 1) % 4) for i in range(4)]
LEFT = [(i, (i + 3) % 4) for i in range(4)]
SWAP = [(0, 1), (1, 0)]
ACROSS = [(0, 3), (3, 0), (1, 2), (2, 1)]
bar = lax.optimization_barrier


def gains(gain_q, gain_k):
    return jnp.tile(gain_q * gain_k * (HD ** -0.5 * 1.4426950408889634), HEADS).reshape(1, D)


def across(v):
    return lax.ppermute(v, ("zh", "zl"), ACROSS)


def swap(v):
    return lax.ppermute(v, "c", SWAP)


def in_pairs(v, axis, other):
    first = lax.axis_index(axis) == 0
    return jnp.concatenate([jnp.where(first, v, other), jnp.where(first, other, v)], 1)


def along_y(quad):
    return quad, lax.ppermute(quad, "y", RIGHT), lax.ppermute(quad, "y", [(i, (i + 2) % 4) for i in range(4)]), lax.ppermute(quad, "y", LEFT)


def in_order(steps):
    y = lax.axis_index("y")
    steps = jnp.stack(steps)
    return jnp.concatenate([lax.dynamic_index_in_dim(steps, lax.rem(y - i + 4, 4), 0, keepdims=False) for i in range(4)], 1)


def per_device(tokens, frame_valid, text, modulation, qk_gains, spatial_qkv, spatial_out, block_weights, cross_kv):
    core, y = lax.axis_index("c"), lax.axis_index("y")
    own = lax.all_to_all(tokens, YZ, 0, 0, tiled=True).reshape(-1, D)
    w1 = lax.dynamic_slice(block_weights, (64 * core, D * y), (HALF, D))
    w2 = lax.dynamic_slice(block_weights, (64 * core, 4 * D), (HALF, 2 * D))
    both1 = jnp.stack([w1, across(w1)])
    local = jnp.dot(text, cross_kv.reshape(D, 2 * HD), preferred_element_type=F32).astype(BF)
    gain_s = gains(qk_gains[0], qk_gains[1])
    gain_t = gains(qk_gains[2], qk_gains[3])
    count = jnp.sum((frame_valid > 0).astype(jnp.int32))
    place = jnp.stack([lax.axis_index("zh"), core, count]).astype(jnp.int32)
    gathered1 = lax.all_gather(both1, ("x", "y", "c"), axis=0)
    pair = in_pairs(local, "c", swap(local))
    own, pair, w2, gain_s, gain_t, place = bar((own, pair, w2, gain_s, gain_t, place))

    other = swap(own)
    besides = lax.ppermute(pair, "zl", SWAP)
    z2 = across(w2)
    after_spatial = spatial(own, other, spatial_qkv, spatial_out, modulation, gain_s)
    after_spatial, besides, z2 = bar((after_spatial, besides, z2))

    rows = lax.all_to_all(after_spatial.reshape(64, 8, D), YZ + XZ, 0, 0, tiled=True).reshape(-1, D)
    steps = along_y(in_pairs(pair, "zl", besides))
    _, both2 = bar((rows, jnp.stack([w2, z2])))
    gathered2 = lax.all_gather(both2, ("x", "c"), axis=0)
    after_temporal = temporal(place, gathered1, rows, modulation, gain_t)
    after_temporal, steps = bar((after_temporal, steps))

    every = in_order(steps).reshape(TEXT, HEADS, 2, HD)
    tk = jnp.pad(every[:, :, 0].reshape(TEXT, D), ((0, TPAD - TEXT), (0, 0)), mode="edge")
    tvt = jnp.pad(every[:, :, 1].reshape(TEXT, D).T, ((0, 0), (0, TPAD - TEXT))).astype(F32)
    back = lax.all_to_all(after_temporal.reshape(8, 64, D), XZ, 0, 0, tiled=True).reshape(-1, D)
    return cross(place, gathered2, back, tk, tvt)


def solution(mesh):
    fine = Mesh(np.asarray(mesh.devices).reshape(4, 2, 4, 2, 2), ("x", "zh", "y", "zl", "c"))
    pos = ("y", "zl", "c")
    placed = (P(XZ, pos, None), P(), P(), P(), P(), P(), P(XZ, None), P(None, None, pos))
    placed = placed[:6] + (P(),) + placed[6:]
    return jax.shard_map(per_device, mesh=fine, in_specs=placed, out_specs=P(XZ, pos, None), check_vma=False)
```

```python
import functools
import jax
import jax.numpy as jnp
from jax import lax
from jax.experimental import pallas as pl
from jax.experimental.pallas import tpu as pltpu

D = 1152
HD = 72
HEADS = 16
WIN = 256
TEXT = 300
TPAD = 304
SHARD = 144
HALF = 80
SAFE = 96.0
BF = jnp.bfloat16
F32 = jnp.float32


def dot(a, b):
    return jnp.dot(a, b, preferred_element_type=F32)


def indicators():
    feature = lax.broadcasted_iota(jnp.int32, (D, 128), 0)
    low = lax.broadcasted_iota(jnp.int32, (D, 128), 1) * HD
    gather = ((feature >= low) & (feature < low + HD)).astype(F32).astype(BF)
    feature = lax.broadcasted_iota(jnp.int32, (256, D), 1)
    low = lax.rem(lax.broadcasted_iota(jnp.int32, (256, D), 0), 128) * HD
    spread = ((feature >= low) & (feature < low + HD)).astype(F32).astype(BF)
    return gather, spread


def norm_rows(x, shift, scale):
    mean = jnp.mean(x, -1, keepdims=True)
    centred = x - mean
    r = lax.rsqrt(jnp.mean(centred * centred, -1, keepdims=True) + 1e-6)
    return (centred * r * (1.0 + scale) + shift).astype(BF)


def head_norm_rows(u, gather, spread, gain):
    total = dot((u * u).astype(BF), gather)
    r = lax.rsqrt(total * (1.0 / HD) + 1e-6)
    high = r.astype(BF)
    low = (r - high.astype(F32)).astype(BF)
    return (u * dot(jnp.concatenate([high, low], -1), spread) * gain).astype(BF)


def window_of(h):
    start = jnp.minimum((h * HD) // 128 * 128, D - WIN)
    return pl.multiple_of(start, 128), h * HD - start


def head_rows(h):
    return pl.ds(pl.multiple_of(h * HD, 8), HD)


def query_of(qt, h, normed):
    start, off = window_of(h)
    win = pl.ds(start, WIN)
    row = lax.broadcasted_iota(jnp.int32, (WIN, 1), 0)
    mine = (row >= off) & (row < off + HD)
    own = qt[head_rows(h), :]
    if not normed:
        return jnp.where(mine, qt[win, :], 0.0).astype(BF)
    r = lax.rsqrt(jnp.sum(own * own, 0, keepdims=True) * (1.0 / HD) + 1e-6)
    return (jnp.where(mine, qt[win, :], 0.0) * r).astype(BF)


def softmax(s, shifted):
    if shifted:
        s = s - jnp.max(s, 0, keepdims=True)
    return jnp.exp2(s).astype(BF)


def values_of(vt, h, cols):
    v = vt[head_rows(h), cols].astype(BF)
    return jnp.concatenate([v, jnp.ones((8, v.shape[1]), BF)], 0)


def loop(n, body):
    def step(i, carry):
        body(i)
        return carry

    lax.fori_loop(0, n, step, 0)


def guarded(gain, run):
    bound = jnp.max(gain[...]) * HD

    @pl.when(bound <= SAFE)
    def _():
        run(False)

    @pl.when(bound > SAFE)
    def _():
        run(True)


def spatial_kernel(own_hbm, other_hbm, wqkv_hbm, wout_hbm, mod, gain, out, own, other, wqkv, wout, xin, k, qt, vt, at, sems, *, rows):
    copies = [pltpu.make_async_copy(own_hbm, own, sems.at[0]), pltpu.make_async_copy(other_hbm, other, sems.at[1])]
    for i in range(3):
        columns = pl.ds(D * i, D)
        copies.append(pltpu.make_async_copy(wqkv_hbm.at[:, columns], wqkv.at[:, columns], sems.at[2 + i]))
    copies.append(pltpu.make_async_copy(wout_hbm, wout, sems.at[5]))
    for copy in copies:
        copy.start()
    gather, spread = indicators()
    shift, scale, gate = mod[0:1, :], mod[1:2, :], mod[2:3, :]
    R = 256

    def block(i):
        return pl.ds(pl.multiple_of(i * R, R), R)

    def normed(i):
        sl, far = block(i), block(i + rows // R)
        xin[sl, :] = norm_rows(own[sl, :].astype(F32), shift, scale)
        xin[far, :] = norm_rows(other[sl, :].astype(F32), shift, scale)

    def project(i):
        sl, far = block(i), block(i + rows // R)
        qt[:, sl] = dot(xin[sl, :], wqkv[:, 0:D]).T
        for to in (sl, far):
            k[to, :] = head_norm_rows(dot(xin[to, :], wqkv[:, D:2 * D]), gather, spread, gain[...])
            vt[:, to] = dot(xin[to, :], wqkv[:, 2 * D:]).T

    for copy in copies[:2]:
        copy.wait()
    loop(rows // R, normed)
    for copy in copies[2:5]:
        copy.wait()
    loop(rows // R, project)

    def run(shifted):
        def heads(i):
            for h in [i] if shifted else [4 * i + j for j in range(4)]:
                start, _ = window_of(h)
                q = query_of(qt, h, True)
                p = softmax(dot(k[:, pl.ds(start, WIN)], q), shifted)
                o = dot(values_of(vt, h, slice(None)), p)
                at[head_rows(h), :] = o[:HD] * (1.0 / o[HD:HD + 1])

        loop(HEADS if shifted else HEADS // 4, heads)

    guarded(gain, run)

    def finish(i):
        sl = block(i)
        proj = dot(at[:, sl].T.astype(BF), wout[...])
        out[sl, :] = (own[sl, :].astype(F32) + gate * proj).astype(BF)

    copies[5].wait()
    loop(rows // R, finish)


VMEM = pl.BlockSpec(memory_space=pltpu.VMEM)
HBM = pl.BlockSpec(memory_space=pl.ANY)
PARAMS = pltpu.CompilerParams(vmem_limit_bytes=60 * 2**20)


def spatial(own, other, wqkv, wout, mod, gain):
    rows = own.shape[0]
    return pl.pallas_call(
        functools.partial(spatial_kernel, rows=rows),
        out_shape=jax.ShapeDtypeStruct((rows, D), BF),
        in_specs=[HBM] * 4 + [VMEM] * 2,
        out_specs=VMEM,
        scratch_shapes=[
            pltpu.VMEM((rows, D), BF),
            pltpu.VMEM((rows, D), BF),
            pltpu.VMEM((D, 3 * D), BF),
            pltpu.VMEM((D, D), BF),
            pltpu.VMEM((2 * rows, D), BF),
            pltpu.VMEM((2 * rows, D), BF),
            pltpu.VMEM((D, rows), F32),
            pltpu.VMEM((D, 2 * rows), F32),
            pltpu.VMEM((D, rows), F32),
            pltpu.SemaphoreType.DMA((6,)),
        ],
        compiler_params=PARAMS,
        cost_estimate=pl.CostEstimate(flops=3 * 10**10, bytes_accessed=2 * 10**7, transcendentals=0),
        name="spatial",
    )(own, other, wqkv, wout, mod, gain)


def piece_copies(place, gathered, weight, sems):
    z = place[0]
    parts = weight.shape[1] // gathered.shape[3]
    copies = []
    for column in range(0, weight.shape[1], D):
        y, at = divmod(column, gathered.shape[3])
        for x in range(4):
            for core in range(2):
                low, count = (0, HALF) if core == 0 else (HALF - 64, 64)
                for dz in range(2):
                    shard = 2 * x + (z if dz == 0 else 1 - z)
                    row = pl.multiple_of(shard * SHARD + core * HALF, 16)
                    dst = weight.at[pl.ds(row, count), pl.ds(column, D)]
                    src = gathered.at[(x * parts + y) * 2 + core, dz, pl.ds(low, count), pl.ds(at, D)]
                    copies.append(pltpu.make_async_copy(src, dst, sems.at[len(copies)]))
    return copies


def ordered(rows, source_of):
    to = lax.broadcasted_iota(jnp.int32, (rows, rows), 0)
    source = lax.broadcasted_iota(jnp.int32, (rows, rows), 1)
    return (source == source_of(to)).astype(F32).astype(BF)


def temporal_kernel(place, gathered, x, mod, gain, out, w, xp, xin, k, qt, vt, at, sems, *, rows, frames):
    copies = piece_copies(place, gathered, w, sems)
    for copy in copies:
        copy.start()
    gather, spread = indicators()
    places = rows // frames
    shift, scale, gate = mod[3:4, :], mod[4:5, :], mod[5:6, :]
    R = 256
    order = ordered(rows, lambda to: lax.rem(to, frames) * places + to // frames)
    for b in range(rows // R):
        sl = pl.ds(b * R, R)
        moved = dot(order[b * R:(b + 1) * R, :], x[...])
        xp[sl, :] = moved.astype(BF)
        xin[sl, :] = norm_rows(moved, shift, scale)
    for copy in copies[:48]:
        copy.wait()
    for b in range(rows // R):
        sl = pl.ds(b * R, R)
        qt[:, sl] = dot(xin[sl, :], w[:, 0:D]).T
        k[sl, :] = head_norm_rows(dot(xin[sl, :], w[:, D:2 * D]), gather, spread, gain[...])
        vt[:, sl] = dot(xin[sl, :], w[:, 2 * D:3 * D]).T

    row = lax.broadcasted_iota(jnp.int32, (R, R), 0)
    held = lax.rem(row, frames)
    frame = lax.rem(held, frames // 8) * 8 + held // (frames // 8)
    query = lax.broadcasted_iota(jnp.int32, (R, R), 1) // frames
    bias = jnp.where((row // frames == query) & (frame < place[2]), 0.0, -1e30)

    def run(shifted):
        def heads(i):
            for h in [i] if shifted else [4 * i + j for j in range(4)]:
                start, _ = window_of(h)
                q = query_of(qt, h, True)
                for b in range(rows // R):
                    sl = pl.ds(b * R, R)
                    s = dot(k[sl, pl.ds(start, WIN)], q[:, b * R:(b + 1) * R]) + bias
                    o = dot(values_of(vt, h, sl), softmax(s, shifted))
                    at[head_rows(h), sl] = o[:HD] * (1.0 / o[HD:HD + 1])

        loop(HEADS if shifted else HEADS // 4, heads)

    guarded(gain, run)
    for copy in copies[48:]:
        copy.wait()
    for b in range(rows // R):
        sl = pl.ds(b * R, R)
        proj = dot(at[:, sl].T.astype(BF), w[:, 3 * D:])
        xin[sl, :] = (xp[sl, :].astype(F32) + gate * proj).astype(BF)
    groups = frames // 8

    def source_of(to):
        place, frame = lax.rem(to, places), to // places
        return place * frames + lax.rem(frame, 8) * groups + frame // 8

    order = ordered(rows, source_of)
    for b in range(rows // R):
        out[pl.ds(b * R, R), :] = dot(order[b * R:(b + 1) * R, :], xin[...]).astype(BF)


def temporal(place, gathered, x, mod, gain):
    rows = x.shape[0]
    return pl.pallas_call(
        functools.partial(temporal_kernel, rows=rows, frames=64),
        out_shape=jax.ShapeDtypeStruct((rows, D), BF),
        in_specs=[pl.BlockSpec(memory_space=pltpu.SMEM)] + [HBM] + [VMEM] * 3,
        out_specs=VMEM,
        scratch_shapes=[
            pltpu.VMEM((D, 4 * D), BF),
            pltpu.VMEM((rows, D), BF),
            pltpu.VMEM((rows, D), BF),
            pltpu.VMEM((rows, D), BF),
            pltpu.VMEM((D, rows), F32),
            pltpu.VMEM((D, rows), F32),
            pltpu.VMEM((D, rows), F32),
            pltpu.SemaphoreType.DMA((64,)),
        ],
        compiler_params=PARAMS,
        cost_estimate=pl.CostEstimate(flops=2 * 10**10, bytes_accessed=2 * 10**7, transcendentals=0),
        name="temporal",
    )(place, gathered, x, mod, gain)


def cross_kernel(place, gathered, x, tk, tvt, out, w, qt, at, sems):
    copies = piece_copies(place, gathered, w, sems)
    for copy in copies:
        copy.start()
    rows = x.shape[0]
    R = 256
    for copy in copies[:16]:
        copy.wait()
    for b in range(rows // R):
        sl = pl.ds(b * R, R)
        cq = dot(x[sl, :], w[:, :D]).astype(BF).astype(F32) * (HD ** -0.5 * 1.4426950408889634)
        qt[:, sl] = cq.T
    lane = lax.broadcasted_iota(jnp.int32, (8, TPAD), 1)
    ones = (lane < TEXT).astype(F32).astype(BF)

    def heads(i):
        for h in [4 * i + j for j in range(4)]:
            start, _ = window_of(h)
            q = query_of(qt, h, False)
            p = softmax(dot(tk[:, pl.ds(start, WIN)], q), True)
            v = jnp.concatenate([tvt[head_rows(h), :].astype(BF), ones], 0)
            o = dot(v, p)
            at[head_rows(h), :] = o[:HD] * (1.0 / o[HD:HD + 1])

    loop(HEADS // 4, heads)
    for copy in copies[16:]:
        copy.wait()
    for b in range(rows // R):
        sl = pl.ds(b * R, R)
        mixed = x[sl, :].astype(F32) + dot(at[:, sl].T.astype(BF), w[:, D:])
        for g in range(R // 64):
            for f in range(8):
                low = g * 64 + f * 8
                out[f, pl.ds((b * (R // 64) + g) * 8, 8), :] = mixed[low:low + 8, :].astype(BF)


def cross(place, gathered, x, tk, tvt):
    rows = x.shape[0]
    return pl.pallas_call(
        cross_kernel,
        out_shape=jax.ShapeDtypeStruct((8, rows // 8, D), BF),
        in_specs=[pl.BlockSpec(memory_space=pltpu.SMEM)] + [HBM] + [VMEM] * 3,
        out_specs=VMEM,
        scratch_shapes=[
            pltpu.VMEM((D, 2 * D), BF),
            pltpu.VMEM((D, rows), F32),
            pltpu.VMEM((D, rows), F32),
            pltpu.SemaphoreType.DMA((64,)),
        ],
        compiler_params=PARAMS,
        cost_estimate=pl.CostEstimate(flops=2 * 10**10, bytes_accessed=2 * 10**7, transcendentals=0),
        name="cross",
    )(place, gathered, x, tk, tvt)


import numpy as np
from jax.sharding import Mesh, PartitionSpec as P

XZ = ("x", "zh")
YZ = ("y", "zl")
RIGHT = [(i, (i + 1) % 4) for i in range(4)]
LEFT = [(i, (i + 3) % 4) for i in range(4)]
SWAP = [(0, 1), (1, 0)]
ACROSS = [(0, 3), (3, 0), (1, 2), (2, 1)]
bar = lax.optimization_barrier


def gains(gain_q, gain_k):
    return jnp.tile(gain_q * gain_k * (HD ** -0.5 * 1.4426950408889634), HEADS).reshape(1, D)


def across(v):
    return lax.ppermute(v, ("zh", "zl"), ACROSS)


def swap(v):
    return lax.ppermute(v, "c", SWAP)


def in_pairs(v, axis, other):
    first = lax.axis_index(axis) == 0
    return jnp.concatenate([jnp.where(first, v, other), jnp.where(first, other, v)], 1)


def along_y(quad):
    return quad, lax.ppermute(quad, "y", RIGHT), lax.ppermute(quad, "y", [(i, (i + 2) % 4) for i in range(4)]), lax.ppermute(quad, "y", LEFT)


def in_order(steps):
    y = lax.axis_index("y")
    steps = jnp.stack(steps)
    return jnp.concatenate([lax.dynamic_index_in_dim(steps, lax.rem(y - i + 4, 4), 0, keepdims=False) for i in range(4)], 1)


def per_device(tokens, frame_valid, text, modulation, qk_gains, spatial_qkv, spatial_out, block_weights, cross_kv):
    core, y = lax.axis_index("c"), lax.axis_index("y")
    own = lax.all_to_all(tokens, YZ, 0, 0, tiled=True).reshape(-1, D)
    w1 = lax.dynamic_slice(block_weights, (64 * core, D * y), (HALF, D))
    w2 = lax.dynamic_slice(block_weights, (64 * core, 4 * D), (HALF, 2 * D))
    both1 = jnp.stack([w1, across(w1)])
    local = jnp.dot(text, cross_kv.reshape(D, 2 * HD), preferred_element_type=F32).astype(BF)
    gain_s = gains(qk_gains[0], qk_gains[1])
    gain_t = gains(qk_gains[2], qk_gains[3])
    count = jnp.sum((frame_valid > 0).astype(jnp.int32))
    place = jnp.stack([lax.axis_index("zh"), core, count]).astype(jnp.int32)
    gathered1 = lax.all_gather(both1, ("x", "y", "c"), axis=0)
    pair = in_pairs(local, "c", swap(local))
    own, pair, w2, gain_s, gain_t, place = bar((own, pair, w2, gain_s, gain_t, place))

    other = swap(own)
    besides = lax.ppermute(pair, "zl", SWAP)
    z2 = across(w2)
    after_spatial = spatial(own, other, spatial_qkv, spatial_out, modulation, gain_s)
    after_spatial, besides, z2 = bar((after_spatial, besides, z2))

    rows = lax.all_to_all(after_spatial.reshape(64, 8, D), YZ + XZ, 0, 0, tiled=True).reshape(-1, D)
    steps = along_y(in_pairs(pair, "zl", besides))
    _, both2 = bar((rows, jnp.stack([w2, z2])))
    gathered2 = lax.all_gather(both2, ("x", "c"), axis=0)
    after_temporal = temporal(place, gathered1, rows, modulation, gain_t)
    after_temporal, steps = bar((after_temporal, steps))

    every = in_order(steps).reshape(TEXT, HEADS, 2, HD)
    tk = jnp.pad(every[:, :, 0].reshape(TEXT, D), ((0, TPAD - TEXT), (0, 0)), mode="edge")
    tvt = jnp.pad(every[:, :, 1].reshape(TEXT, D).T, ((0, 0), (0, TPAD - TEXT))).astype(F32)
    back = lax.all_to_all(after_temporal.reshape(8, 64, D), XZ, 0, 0, tiled=True).reshape(-1, D)
    return cross(place, gathered2, back, tk, tvt)


def solution(mesh):
    fine = Mesh(np.asarray(mesh.devices).reshape(4, 2, 4, 2, 2), ("x", "zh", "y", "zl", "c"))
    pos = ("y", "zl", "c")
    placed = (P(XZ, pos, None), P(), P(), P(), P(), P(), P(XZ, None), P(None, None, pos))
    placed = placed[:6] + (P(),) + placed[6:]
    return jax.shard_map(per_device, mesh=fine, in_specs=placed, out_specs=P(XZ, pos, None), check_vma=False)
```

```python
import functools
import jax
import jax.numpy as jnp
from jax import lax
from jax.experimental import pallas as pl
from jax.experimental.pallas import tpu as pltpu

D = 1152
HD = 72
HEADS = 16
WIN = 256
TEXT = 300
TPAD = 304
SHARD = 144
HALF = 80
SAFE = 96.0
BF = jnp.bfloat16
F32 = jnp.float32


def dot(a, b):
    return jnp.dot(a, b, preferred_element_type=F32)


def indicators():
    feature = lax.broadcasted_iota(jnp.int32, (D, 128), 0)
    low = lax.broadcasted_iota(jnp.int32, (D, 128), 1) * HD
    gather = ((feature >= low) & (feature < low + HD)).astype(F32).astype(BF)
    feature = lax.broadcasted_iota(jnp.int32, (256, D), 1)
    low = lax.rem(lax.broadcasted_iota(jnp.int32, (256, D), 0), 128) * HD
    spread = ((feature >= low) & (feature < low + HD)).astype(F32).astype(BF)
    return gather, spread


def norm_rows(x, shift, scale):
    mean = jnp.mean(x, -1, keepdims=True)
    centred = x - mean
    r = lax.rsqrt(jnp.mean(centred * centred, -1, keepdims=True) + 1e-6)
    return (centred * r * (1.0 + scale) + shift).astype(BF)


def head_norm_rows(u, gather, spread, gain):
    total = dot((u * u).astype(BF), gather)
    r = lax.rsqrt(total * (1.0 / HD) + 1e-6)
    high = r.astype(BF)
    low = (r - high.astype(F32)).astype(BF)
    return (u * dot(jnp.concatenate([high, low], -1), spread) * gain).astype(BF)


def window_of(h):
    start = jnp.minimum((h * HD) // 128 * 128, D - WIN)
    return pl.multiple_of(start, 128), h * HD - start


def head_rows(h):
    return pl.ds(pl.multiple_of(h * HD, 8), HD)


def query_of(qt, h, normed):
    start, off = window_of(h)
    win = pl.ds(start, WIN)
    row = lax.broadcasted_iota(jnp.int32, (WIN, 1), 0)
    mine = (row >= off) & (row < off + HD)
    own = qt[head_rows(h), :]
    if not normed:
        return jnp.where(mine, qt[win, :], 0.0).astype(BF)
    r = lax.rsqrt(jnp.sum(own * own, 0, keepdims=True) * (1.0 / HD) + 1e-6)
    return (jnp.where(mine, qt[win, :], 0.0) * r).astype(BF)


def softmax(s, shifted):
    if shifted:
        s = s - jnp.max(s, 0, keepdims=True)
    return jnp.exp2(s).astype(BF)


def values_of(vt, h, cols):
    v = vt[head_rows(h), cols].astype(BF)
    return jnp.concatenate([v, jnp.ones((8, v.shape[1]), BF)], 0)


def loop(n, body):
    def step(i, carry):
        body(i)
        return carry

    lax.fori_loop(0, n, step, 0)


def guarded(gain, run):
    bound = jnp.max(gain[...]) * HD

    @pl.when(bound <= SAFE)
    def _():
        run(False)

    @pl.when(bound > SAFE)
    def _():
        run(True)


def spatial_kernel(own_hbm, other_hbm, wqkv_hbm, wout_hbm, mod, gain, out, own, other, wqkv, wout, xin, k, qt, vt, at, sems, *, rows):
    copies = [pltpu.make_async_copy(own_hbm, own, sems.at[0]), pltpu.make_async_copy(other_hbm, other, sems.at[1])]
    for i in range(3):
        columns = pl.ds(D * i, D)
        copies.append(pltpu.make_async_copy(wqkv_hbm.at[:, columns], wqkv.at[:, columns], sems.at[2 + i]))
    copies.append(pltpu.make_async_copy(wout_hbm, wout, sems.at[5]))
    for copy in copies:
        copy.start()
    gather, spread = indicators()
    shift, scale, gate = mod[0:1, :], mod[1:2, :], mod[2:3, :]
    R = 256

    def block(i):
        return pl.ds(pl.multiple_of(i * R, R), R)

    def normed(i):
        sl, far = block(i), block(i + rows // R)
        xin[sl, :] = norm_rows(own[sl, :].astype(F32), shift, scale)
        xin[far, :] = norm_rows(other[sl, :].astype(F32), shift, scale)

    def project(i):
        sl, far = block(i), block(i + rows // R)
        qt[:, sl] = dot(xin[sl, :], wqkv[:, 0:D]).T
        for to in (sl, far):
            k[to, :] = head_norm_rows(dot(xin[to, :], wqkv[:, D:2 * D]), gather, spread, gain[...])
            vt[:, to] = dot(xin[to, :], wqkv[:, 2 * D:]).T

    for copy in copies[:2]:
        copy.wait()
    loop(rows // R, normed)
    for copy in copies[2:5]:
        copy.wait()
    loop(rows // R, project)

    def run(shifted):
        def heads(i):
            for h in [i] if shifted else [4 * i + j for j in range(4)]:
                start, _ = window_of(h)
                q = query_of(qt, h, True)
                p = softmax(dot(k[:, pl.ds(start, WIN)], q), shifted)
                o = dot(values_of(vt, h, slice(None)), p)
                at[head_rows(h), :] = o[:HD] * (1.0 / o[HD:HD + 1])

        loop(HEADS if shifted else HEADS // 4, heads)

    guarded(gain, run)

    def finish(i):
        sl = block(i)
        proj = dot(at[:, sl].T.astype(BF), wout[...])
        out[sl, :] = (own[sl, :].astype(F32) + gate * proj).astype(BF)

    copies[5].wait()
    loop(rows // R, finish)


VMEM = pl.BlockSpec(memory_space=pltpu.VMEM)
HBM = pl.BlockSpec(memory_space=pl.ANY)
PARAMS = pltpu.CompilerParams(vmem_limit_bytes=60 * 2**20)


def spatial(own, other, wqkv, wout, mod, gain):
    rows = own.shape[0]
    return pl.pallas_call(
        functools.partial(spatial_kernel, rows=rows),
        out_shape=jax.ShapeDtypeStruct((rows, D), BF),
        in_specs=[HBM] * 4 + [VMEM] * 2,
        out_specs=VMEM,
        scratch_shapes=[
            pltpu.VMEM((rows, D), BF),
            pltpu.VMEM((rows, D), BF),
            pltpu.VMEM((D, 3 * D), BF),
            pltpu.VMEM((D, D), BF),
            pltpu.VMEM((2 * rows, D), BF),
            pltpu.VMEM((2 * rows, D), BF),
            pltpu.VMEM((D, rows), F32),
            pltpu.VMEM((D, 2 * rows), F32),
            pltpu.VMEM((D, rows), F32),
            pltpu.SemaphoreType.DMA((6,)),
        ],
        compiler_params=PARAMS,
        cost_estimate=pl.CostEstimate(flops=3 * 10**10, bytes_accessed=2 * 10**7, transcendentals=0),
        name="spatial",
    )(own, other, wqkv, wout, mod, gain)


def piece_copies(place, gathered, weight, sems):
    z = place[0]
    parts = weight.shape[1] // gathered.shape[3]
    copies = []
    for column in range(0, weight.shape[1], D):
        y, at = divmod(column, gathered.shape[3])
        for x in range(4):
            for core in range(2):
                low, count = (0, HALF) if core == 0 else (HALF - 64, 64)
                for dz in range(2):
                    shard = 2 * x + (z if dz == 0 else 1 - z)
                    row = pl.multiple_of(shard * SHARD + core * HALF, 16)
                    dst = weight.at[pl.ds(row, count), pl.ds(column, D)]
                    src = gathered.at[(x * parts + y) * 2 + core, dz, pl.ds(low, count), pl.ds(at, D)]
                    copies.append(pltpu.make_async_copy(src, dst, sems.at[len(copies)]))
    return copies


def ordered(rows, source_of):
    to = lax.broadcasted_iota(jnp.int32, (rows, rows), 0)
    source = lax.broadcasted_iota(jnp.int32, (rows, rows), 1)
    return (source == source_of(to)).astype(F32).astype(BF)


def temporal_kernel(place, gathered, x, mod, gain, out, w, xp, xin, k, qt, vt, at, sems, *, rows, frames):
    copies = piece_copies(place, gathered, w, sems)
    for copy in copies:
        copy.start()
    gather, spread = indicators()
    places = rows // frames
    shift, scale, gate = mod[3:4, :], mod[4:5, :], mod[5:6, :]
    R = 256
    order = ordered(rows, lambda to: lax.rem(to, frames) * places + to // frames)
    for b in range(rows // R):
        sl = pl.ds(b * R, R)
        moved = dot(order[b * R:(b + 1) * R, :], x[...])
        xp[sl, :] = moved.astype(BF)
        xin[sl, :] = norm_rows(moved, shift, scale)
    for copy in copies[:48]:
        copy.wait()
    for b in range(rows // R):
        sl = pl.ds(b * R, R)
        qt[:, sl] = dot(xin[sl, :], w[:, 0:D]).T
        k[sl, :] = head_norm_rows(dot(xin[sl, :], w[:, D:2 * D]), gather, spread, gain[...])
        vt[:, sl] = dot(xin[sl, :], w[:, 2 * D:3 * D]).T

    row = lax.broadcasted_iota(jnp.int32, (R, R), 0)
    held = lax.rem(row, frames)
    frame = lax.rem(held, frames // 8) * 8 + held // (frames // 8)
    query = lax.broadcasted_iota(jnp.int32, (R, R), 1) // frames
    bias = jnp.where((row // frames == query) & (frame < place[2]), 0.0, -1e30)

    def run(shifted):
        def heads(i):
            for h in [i] if shifted else [4 * i + j for j in range(4)]:
                start, _ = window_of(h)
                q = query_of(qt, h, True)
                for b in range(rows // R):
                    sl = pl.ds(b * R, R)
                    s = dot(k[sl, pl.ds(start, WIN)], q[:, b * R:(b + 1) * R]) + bias
                    o = dot(values_of(vt, h, sl), softmax(s, shifted))
                    at[head_rows(h), sl] = o[:HD] * (1.0 / o[HD:HD + 1])

        loop(HEADS if shifted else HEADS // 4, heads)

    guarded(gain, run)
    for copy in copies[48:]:
        copy.wait()
    for b in range(rows // R):
        sl = pl.ds(b * R, R)
        proj = dot(at[:, sl].T.astype(BF), w[:, 3 * D:])
        xin[sl, :] = (xp[sl, :].astype(F32) + gate * proj).astype(BF)
    groups = frames // 8

    def source_of(to):
        place, frame = lax.rem(to, places), to // places
        return place * frames + lax.rem(frame, 8) * groups + frame // 8

    order = ordered(rows, source_of)
    for b in range(rows // R):
        out[pl.ds(b * R, R), :] = dot(order[b * R:(b + 1) * R, :], xin[...]).astype(BF)


def temporal(place, gathered, x, mod, gain):
    rows = x.shape[0]
    return pl.pallas_call(
        functools.partial(temporal_kernel, rows=rows, frames=64),
        out_shape=jax.ShapeDtypeStruct((rows, D), BF),
        in_specs=[pl.BlockSpec(memory_space=pltpu.SMEM)] + [HBM] + [VMEM] * 3,
        out_specs=VMEM,
        scratch_shapes=[
            pltpu.VMEM((D, 4 * D), BF),
            pltpu.VMEM((rows, D), BF),
            pltpu.VMEM((rows, D), BF),
            pltpu.VMEM((rows, D), BF),
            pltpu.VMEM((D, rows), F32),
            pltpu.VMEM((D, rows), F32),
            pltpu.VMEM((D, rows), F32),
            pltpu.SemaphoreType.DMA((64,)),
        ],
        compiler_params=PARAMS,
        cost_estimate=pl.CostEstimate(flops=2 * 10**10, bytes_accessed=2 * 10**7, transcendentals=0),
        name="temporal",
    )(place, gathered, x, mod, gain)


def cross_kernel(place, gathered, x, tk, tvt, out, w, qt, at, sems):
    copies = piece_copies(place, gathered, w, sems)
    for copy in copies:
        copy.start()
    rows = x.shape[0]
    R = 256
    for copy in copies[:16]:
        copy.wait()
    for b in range(rows // R):
        sl = pl.ds(b * R, R)
        cq = dot(x[sl, :], w[:, :D]).astype(BF).astype(F32) * (HD ** -0.5 * 1.4426950408889634)
        qt[:, sl] = cq.T
    lane = lax.broadcasted_iota(jnp.int32, (8, TPAD), 1)
    ones = (lane < TEXT).astype(F32).astype(BF)

    def heads(i):
        for h in [4 * i + j for j in range(4)]:
            start, _ = window_of(h)
            q = query_of(qt, h, False)
            p = softmax(dot(tk[:, pl.ds(start, WIN)], q), True)
            v = jnp.concatenate([tvt[head_rows(h), :].astype(BF), ones], 0)
            o = dot(v, p)
            at[head_rows(h), :] = o[:HD] * (1.0 / o[HD:HD + 1])

    loop(HEADS // 4, heads)
    for copy in copies[16:]:
        copy.wait()
    for b in range(rows // R):
        sl = pl.ds(b * R, R)
        mixed = x[sl, :].astype(F32) + dot(at[:, sl].T.astype(BF), w[:, D:])
        for g in range(0, R // 64, 2):
            for f in range(8):
                low, high = g * 64 + f * 8, (g + 1) * 64 + f * 8
                two = jnp.concatenate([mixed[low:low + 8, :], mixed[high:high + 8, :]], 0)
                out[f, pl.ds((b * (R // 64) + g) * 8, 16), :] = two.astype(BF)


def cross(place, gathered, x, tk, tvt):
    rows = x.shape[0]
    return pl.pallas_call(
        cross_kernel,
        out_shape=jax.ShapeDtypeStruct((8, rows // 8, D), BF),
        in_specs=[pl.BlockSpec(memory_space=pltpu.SMEM)] + [HBM] + [VMEM] * 3,
        out_specs=VMEM,
        scratch_shapes=[
            pltpu.VMEM((D, 2 * D), BF),
            pltpu.VMEM((D, rows), F32),
            pltpu.VMEM((D, rows), F32),
            pltpu.SemaphoreType.DMA((64,)),
        ],
        compiler_params=PARAMS,
        cost_estimate=pl.CostEstimate(flops=2 * 10**10, bytes_accessed=2 * 10**7, transcendentals=0),
        name="cross",
    )(place, gathered, x, tk, tvt)


import numpy as np
from jax.sharding import Mesh, PartitionSpec as P

XZ = ("x", "zh")
YZ = ("y", "zl")
RIGHT = [(i, (i + 1) % 4) for i in range(4)]
LEFT = [(i, (i + 3) % 4) for i in range(4)]
SWAP = [(0, 1), (1, 0)]
ACROSS = [(0, 3), (3, 0), (1, 2), (2, 1)]
bar = lax.optimization_barrier


def gains(gain_q, gain_k):
    return jnp.tile(gain_q * gain_k * (HD ** -0.5 * 1.4426950408889634), HEADS).reshape(1, D)


def across(v):
    return lax.ppermute(v, ("zh", "zl"), ACROSS)


def swap(v):
    return lax.ppermute(v, "c", SWAP)


def in_pairs(v, axis, other):
    first = lax.axis_index(axis) == 0
    return jnp.concatenate([jnp.where(first, v, other), jnp.where(first, other, v)], 1)


def along_y(quad):
    return quad, lax.ppermute(quad, "y", RIGHT), lax.ppermute(quad, "y", [(i, (i + 2) % 4) for i in range(4)]), lax.ppermute(quad, "y", LEFT)


def in_order(steps):
    y = lax.axis_index("y")
    steps = jnp.stack(steps)
    return jnp.concatenate([lax.dynamic_index_in_dim(steps, lax.rem(y - i + 4, 4), 0, keepdims=False) for i in range(4)], 1)


def per_device(tokens, frame_valid, text, modulation, qk_gains, spatial_qkv, spatial_out, block_weights, cross_kv):
    core, y = lax.axis_index("c"), lax.axis_index("y")
    own = lax.all_to_all(tokens, YZ, 0, 0, tiled=True).reshape(-1, D)
    w1 = lax.dynamic_slice(block_weights, (64 * core, D * y), (HALF, D))
    w2 = lax.dynamic_slice(block_weights, (64 * core, 4 * D), (HALF, 2 * D))
    both1 = jnp.stack([w1, across(w1)])
    local = jnp.dot(text, cross_kv.reshape(D, 2 * HD), preferred_element_type=F32).astype(BF)
    gain_s = gains(qk_gains[0], qk_gains[1])
    gain_t = gains(qk_gains[2], qk_gains[3])
    count = jnp.sum((frame_valid > 0).astype(jnp.int32))
    place = jnp.stack([lax.axis_index("zh"), core, count]).astype(jnp.int32)
    gathered1 = lax.all_gather(both1, ("x", "y", "c"), axis=0)
    pair = in_pairs(local, "c", swap(local))
    own, pair, w2, gain_s, gain_t, place = bar((own, pair, w2, gain_s, gain_t, place))

    other = swap(own)
    besides = lax.ppermute(pair, "zl", SWAP)
    z2 = across(w2)
    after_spatial = spatial(own, other, spatial_qkv, spatial_out, modulation, gain_s)
    after_spatial, besides, z2 = bar((after_spatial, besides, z2))

    rows = lax.all_to_all(after_spatial.reshape(64, 8, D), YZ + XZ, 0, 0, tiled=True).reshape(-1, D)
    steps = along_y(in_pairs(pair, "zl", besides))
    _, both2 = bar((rows, jnp.stack([w2, z2])))
    gathered2 = lax.all_gather(both2, ("x", "c"), axis=0)
    after_temporal = temporal(place, gathered1, rows, modulation, gain_t)
    after_temporal, steps = bar((after_temporal, steps))

    every = in_order(steps).reshape(TEXT, HEADS, 2, HD)
    tk = jnp.pad(every[:, :, 0].reshape(TEXT, D), ((0, TPAD - TEXT), (0, 0)), mode="edge")
    tvt = jnp.pad(every[:, :, 1].reshape(TEXT, D).T, ((0, 0), (0, TPAD - TEXT))).astype(F32)
    back = lax.all_to_all(after_temporal.reshape(8, 64, D), XZ, 0, 0, tiled=True).reshape(-1, D)
    return cross(place, gathered2, back, tk, tvt)


def solution(mesh):
    fine = Mesh(np.asarray(mesh.devices).reshape(4, 2, 4, 2, 2), ("x", "zh", "y", "zl", "c"))
    pos = ("y", "zl", "c")
    placed = (P(XZ, pos, None), P(), P(), P(), P(), P(), P(XZ, None), P(None, None, pos))
    placed = placed[:6] + (P(),) + placed[6:]
    return jax.shard_map(per_device, mesh=fine, in_specs=placed, out_specs=P(XZ, pos, None), check_vma=False)
```
